128 devices in a mesh: ctx: 64 (over x, y_lo, z, core), mp: 2 (over y_hi).
Axes of the slice: x: 4, y: 4 (y_hi: 2, y_lo: 2; y = y_hi * 2 + y_lo), z: 4, core: 2. Of those that a mesh axis runs over, the one named last changes fastest.
Arguments:
- inputs: bfloat16 [8192, 2560], P('ctx'), may hold values from -6 to 6
- attn_gain: bfloat16 [2560], P('ctx'), may hold values from 0.099609375 to 1.8984375
- query_weight: bfloat16 [2560, 2560], P('ctx', 'mp'), may hold values from -0.125 to 0.125
- keyval_weight: bfloat16 [2560, 512], P('ctx'), may hold values from -0.125 to 0.125
- out_weight: bfloat16 [2560, 2560], P('mp', 'ctx'), may hold values from -3 to 3
- ffn_gain: bfloat16 [2560], P('ctx'), may hold values from 0.099609375 to 1.8984375
- gate_weight: bfloat16 [2560, 7680], P('ctx', 'mp'), may hold values from -0.125 to 0.125
- up_weight: bfloat16 [2560, 7680], P('ctx', 'mp'), may hold values from -0.125 to 0.125
- down_weight: bfloat16 [7680, 2560], P('mp', 'ctx'), may hold values from -0.0625 to 0.0625
- positions: int32 [8192], replicated, may hold values from 0 to 10239, as said below
- cotangent: bfloat16 [8192, 2560], P('ctx'), may hold values from -6 to 6
Outputs:
- activations: bfloat16 [8192, 2560], P('ctx')
- input_grad: float32 [8192, 2560], P('ctx')
- attn_gain_grad: float32 [2560], P('ctx')
- query_weight_grad: float32 [2560, 2560], P('ctx', 'mp')
- keyval_weight_grad: float32 [2560, 512], P('ctx')
- out_weight_grad: float32 [2560, 2560], P('mp', 'ctx')
- ffn_gain_grad: float32 [2560], P('ctx')
- gate_weight_grad: float32 [2560, 7680], P('ctx', 'mp')
- up_weight_grad: float32 [2560, 7680], P('ctx', 'mp')
- down_weight_grad: float32 [7680, 2560], P('mp', 'ctx')
The draws below stay inside these ranges and needn't reach their ends.
Inputs may be any that keep to these rules, and one draw needn't show every extreme that they name: positions strictly increase along the sequence.
All inputs are finite; a program needn't handle non-finite values.
Results may differ from the reference program's by a relative error of at most 0.017.
Values may be sent and summed in bfloat16 or wider, within the bound.
No kernel may reach another device: no remote copies, remote signals or barrier semaphores. Data moves between devices by JAX's collectives and lax.ppermute only.
A program may use at most 320 MiB of HBM per device.

```python
import jax
import jax.numpy as jnp
from jax import lax

D = 2560
HEADS = 10
HD = 256
FF = 7680
WINDOW = 2048
SEQ = 8192


def draw_positions(key, part):
    key = jax.random.fold_in(key, 5)
    key_place, key_first, key_second = jax.random.split(key, 3)
    places = jax.random.randint(key_place, (3,), 1, SEQ)
    first_gap = jax.random.randint(key_first, (), 1, WINDOW // 2)
    second_gap = jax.random.randint(key_second, (), 1, WINDOW // 2)
    third_gap = WINDOW - first_gap - second_gap
    sizes = jnp.stack([first_gap, second_gap, third_gap]).astype(jnp.int32)
    index_all = jnp.arange(SEQ, dtype=jnp.int32)
    passed = (index_all[:, None] >= places[None, :]).astype(jnp.int32)
    return (index_all + jnp.sum(passed * sizes[None, :], axis=1)).astype(jnp.int32)


def block_scale(rng, extent, cuts, smallest, high):
    def one(position, blocks):
        heights = jax.random.uniform(jax.random.fold_in(jax.random.fold_in(rng, 6), position), (blocks,), jnp.float32, smallest / len(cuts), high / len(cuts))
        return jnp.repeat(jnp.exp(heights), extent[position] // blocks).reshape((-1,) + (1,) * (len(extent) - position - 1))

    loudness = one(*cuts[0])
    for cut in cuts[1:]:
        loudness = loudness * one(*cut)
    return loudness


def gaussian(key, shape, spread, reach, cuts=(), held_as=jnp.bfloat16):
    gain = block_scale(key, shape, cuts, -0.22, 0.18) if cuts else 1.0
    values = jax.random.normal(key, shape, jnp.float32) * spread * gain
    return jnp.minimum(jnp.maximum(values, -reach), reach).astype(held_as)


def setup_inputs(seed: int = 0) -> dict:
    arg_keys = jax.random.split(jax.random.key(seed), 12)
    inputs = gaussian(arg_keys[0], (SEQ, D), 1.0, 6.0, ((0, 64),))
    attn_gain = jnp.clip(1.0 + 0.18 * jax.random.normal(arg_keys[1], (D,), jnp.float32), 0.099609375, 1.8984375).astype(jnp.bfloat16)
    query_weight = gaussian(arg_keys[2], (D, HEADS * HD), D ** -0.5, 0.125, ((0, 64), (1, 2)))
    keyval_weight = gaussian(arg_keys[3], (D, 2 * HD), D ** -0.5, 0.125, ((0, 64),))
    out_weight = gaussian(arg_keys[4], (HEADS * HD, D), 4 ** -0.5, 3.0, ((0, 2), (1, 64)))
    ffn_gain = jnp.clip(1.0 + 0.18 * jax.random.normal(arg_keys[5], (D,), jnp.float32), 0.099609375, 1.8984375).astype(jnp.bfloat16)
    gate_weight = gaussian(arg_keys[6], (D, FF), D ** -0.5, 0.125, ((0, 64), (1, 2)))
    up_weight = gaussian(arg_keys[7], (D, FF), D ** -0.5, 0.125, ((0, 64), (1, 2)))
    down_weight = gaussian(arg_keys[8], (FF, D), FF ** -0.5, 0.0625, ((0, 2), (1, 64)))
    positions = draw_positions(jax.random.fold_in(arg_keys[11], 71), 0)
    cotangent = gaussian(arg_keys[10], (SEQ, D), 1.0, 6.0, ((0, 64),))
    return dict(inputs=inputs, attn_gain=attn_gain, query_weight=query_weight, keyval_weight=keyval_weight, out_weight=out_weight, ffn_gain=ffn_gain, gate_weight=gate_weight, up_weight=up_weight, down_weight=down_weight, positions=positions, cotangent=cotangent)


EPS = 1e-06

@jax.custom_vjp
def low(v):
    return lax.optimization_barrier(v.astype(jnp.bfloat16)).astype(jnp.float32)

@jax.custom_vjp
def low_back(v):
    return v

def low_keep(v):
    return (low(v), None)

def low_pass(kept, grad):
    return (grad,)

def back_keep(v):
    return (v, None)

def back_low(kept, grad):
    return (low(grad),)
low.defvjp(low_keep, low_pass)
low_back.defvjp(back_keep, back_low)

def matmul(left, right):
    return jnp.dot(left, right, precision=lax.Precision.HIGHEST, preferred_element_type=jnp.float32)

def rms_scale(values):
    return lax.rsqrt(lax.optimization_barrier(jnp.mean(values * values, axis=-1, keepdims=True)) + EPS)

def window_block(first_row, query_heads, keys_padded, pos_padded, positions):
    q_rows = WINDOW // 4
    scale = HD ** (-0.5)
    queries = lax.dynamic_slice_in_dim(query_heads, first_row, q_rows, 0)
    keyvals = lax.dynamic_slice_in_dim(keys_padded, first_row, q_rows + WINDOW, 0)
    pos_query = lax.dynamic_slice_in_dim(positions, first_row, q_rows, 0)
    pos_key = lax.dynamic_slice_in_dim(pos_padded, first_row, q_rows + WINDOW, 0)
    query_index = first_row + jnp.arange(q_rows, dtype=jnp.int32)
    key_index = first_row - WINDOW + jnp.arange(q_rows + WINDOW, dtype=jnp.int32)
    allowed = (key_index[None, :] >= 0) & (key_index[None, :] <= query_index[:, None]) & (pos_query[:, None] - pos_key[None, :] < WINDOW)
    raw_scores = jnp.einsum('qhd,kd->hqk', queries, keyvals[:, :HD], precision=lax.Precision.HIGHEST) * scale
    scores = jnp.where(allowed[None], low_back(raw_scores), -1e+30)
    weights = low(jax.nn.softmax(scores, axis=-1))
    attended = jnp.einsum('hqk,kd->qhd', weights, keyvals[:, HD:], precision=lax.Precision.HIGHEST)
    return attended.reshape(q_rows, -1)

def attend(queries, keyvals, positions):
    token_count = queries.shape[0]
    head_count = queries.shape[1] // HD
    q_rows = WINDOW // 4
    query_heads = queries.reshape(token_count, head_count, HD)
    keys_padded = jnp.concatenate([jnp.zeros((WINDOW, 2 * HD), jnp.float32), keyvals], 0)
    pos_padded = jnp.concatenate([jnp.zeros((WINDOW,), jnp.int32), positions.astype(jnp.int32)], 0)
    blocked = jax.checkpoint(window_block)
    starts = (jnp.arange(token_count // q_rows) * q_rows).astype(jnp.int32)
    pieces = lax.map(lambda first_row: blocked(first_row, query_heads, keys_padded, pos_padded, positions), starts)
    return pieces.reshape(token_count, head_count * HD)

def forward(inputs, attn_gain, query_weight, keyval_weight, out_weight, ffn_gain, gate_weight, up_weight, down_weight, positions):
    normed_attn = low(inputs * rms_scale(inputs) * attn_gain)
    queries = low_back(low(matmul(normed_attn, query_weight)))
    keyvals = low_back(low(matmul(normed_attn, keyval_weight)))
    attended = low_back(low(attend(queries, keyvals, positions)))
    middle = inputs + low_back(matmul(attended, out_weight))
    normed_ffn = low(middle * rms_scale(middle) * ffn_gain)
    gate_proj = low_back(matmul(normed_ffn, gate_weight))
    up_proj = low_back(matmul(normed_ffn, up_weight))
    hidden = low_back(low(jax.nn.gelu(gate_proj, approximate=True) * up_proj))
    return middle + low_back(matmul(hidden, down_weight))

def reference(inputs, attn_gain, query_weight, keyval_weight, out_weight, ffn_gain, gate_weight, up_weight, down_weight, positions, cotangent):

    def closed(in_rows, gain_one, w_query, w_keyval, w_out, gain_two, w_gate, w_up, w_down):
        return forward(in_rows, gain_one, w_query, w_keyval, w_out, gain_two, w_gate, w_up, w_down, positions)
    result, pullback = jax.vjp(closed, inputs.astype(jnp.float32), attn_gain.astype(jnp.float32), query_weight.astype(jnp.float32), keyval_weight.astype(jnp.float32), out_weight.astype(jnp.float32), ffn_gain.astype(jnp.float32), gate_weight.astype(jnp.float32), up_weight.astype(jnp.float32), down_weight.astype(jnp.float32))
    grads = pullback(cotangent.astype(jnp.float32))
    return (result.astype(jnp.bfloat16), grads[0], grads[1], grads[2], grads[3], grads[4], grads[5], grads[6], grads[7], grads[8])
```

```python
import functools

import jax
import jax.numpy as jnp
from jax import lax
from jax.experimental import pallas as pl
from jax.experimental.pallas import tpu as pltpu
from jax.sharding import Mesh, PartitionSpec as P

HD = 256
WINDOW = 2048
EPS = 1e-06

PLANES = 4
RANK_SIZES = (2, 4, 2)
RANKS = 16
PARTS = 2
X = "x"
R = ("yl", "z", "c")
M = "mp"

F32 = jnp.float32
BF16 = jnp.bfloat16


def after(value, *earlier):
    return lax.optimization_barrier((value,) + earlier)[0]


def rms_scale(values):
    return lax.rsqrt(jnp.mean(values * values, axis=-1, keepdims=True) + EPS)


def norm_back(values, scale_rows, weighted):
    return scale_rows * weighted - values * scale_rows**3 * jnp.mean(
        weighted * values, axis=-1, keepdims=True
    )


def to_plane(block, shift):
    return lax.ppermute(block, X, [(i, (i + shift) % PLANES) for i in range(PLANES)])


def swap(block):
    return lax.ppermute(block, M, [(0, 1), (1, 0)])


def rounded(values):
    return lax.reduce_precision(values, 8, 7).astype(BF16)


def sum_mp(part):
    low = rounded(part)
    return low.astype(F32) + swap(low).astype(F32)


def gather_planes(block):
    half = block.shape[0] // 2
    after = to_plane(block, -1)
    before = to_plane(block, 1)
    far_top = to_plane(before[:half], 1)
    far_low = to_plane(after[half:], -1)
    return jnp.concatenate([block, after, far_top, far_low, before], 0)


def reduce_planes(part):
    rows = part.shape[0] // PLANES
    half = rows // 2
    own, after, far, before = (part[i * rows : (i + 1) * rows] for i in range(PLANES))
    far = rounded(far)
    top = to_plane(far[:half], 1).astype(F32)
    low = to_plane(far[half:], -1).astype(F32)
    after = jnp.concatenate([after[:half] + top, after[half:]], 0)
    before = jnp.concatenate([before[:half], before[half:] + low], 0)
    return (
        own
        + to_plane(rounded(before), -1).astype(F32)
        + to_plane(rounded(after), 1).astype(F32)
    )


def pick(blocks, index):
    return lax.dynamic_index_in_dim(blocks, lax.rem(index + PLANES, PLANES), 0, keepdims=False)


def natural(blocks):
    plane = lax.axis_index(X)
    return [pick(blocks, p - plane) for p in range(PLANES)]


def send_planes(blocks):
    plane = lax.axis_index(X)
    return [pick(blocks, plane)] + [
        to_plane(pick(blocks, plane + k), k) for k in range(1, PLANES)
    ]


def exchange_planes(blocks):
    plane = lax.axis_index(X)
    got = jnp.stack(send_planes(blocks))
    return [pick(got, plane - p) for p in range(PLANES)]


def cut_planes(values):
    rows, width = values.shape
    got = send_planes(values.reshape(rows, PLANES, width // PLANES).swapaxes(0, 1))
    return jnp.concatenate([got[0], got[3], got[2], got[1]], 0)


def cut_features(blocks):
    got = send_planes(blocks)
    return jnp.concatenate([got[0], got[3], got[2], got[1]], 1)


def join_planes(values):
    blocks = values.reshape(PLANES, values.shape[0] // PLANES, values.shape[1])
    got = jnp.stack([blocks[0]] + [to_plane(blocks[k], k) for k in range(1, PLANES)])
    plane = lax.axis_index(X)
    return jnp.concatenate([pick(got, plane - p) for p in range(PLANES)], 1)


def permute_features(values):
    rows, width = values.shape
    cut = values.reshape(rows, PLANES, RANKS, width // (PLANES * RANKS))
    return cut.swapaxes(1, 2).reshape(rows, width)


def restore_features(values):
    rows, width = values.shape
    cut = values.reshape(rows, RANKS, PLANES, width // (PLANES * RANKS))
    return cut.swapaxes(1, 2).reshape(rows, width)


def spread(block, axes, size):
    rows, columns = block.shape
    copies = jnp.broadcast_to(block[None], (size, rows, columns)).reshape(size * rows, columns)
    return lax.all_to_all(copies, axes, 0, 0, tiled=True)


def gather_rows(block):
    return lax.all_gather(block, R, axis=0, tiled=True)


def dot_rows(left, right):
    return lax.dot_general(left, right, (((1,), (1,)), ((), ())), preferred_element_type=F32)


def dot_tokens(left, right):
    return lax.dot_general(left, right, (((0,), (0,)), ((), ())), preferred_element_type=F32)


def softmax_parts(query, parts, biases):
    scale = HD ** (-0.5)
    scores = [dot_rows(query, part[0]) * scale + bias[...] for part, bias in zip(parts, biases)]
    top = functools.reduce(
        jnp.maximum, [jnp.max(score, axis=-1, keepdims=True) for score in scores]
    )
    scores = [jnp.exp(score - top) for score in scores]
    inverse = 1.0 / sum(jnp.sum(score, axis=-1, keepdims=True) for score in scores)
    return [score * inverse for score in scores]


def attend_kernel(count, query, *refs):
    parts, biases, out = refs[:count], refs[count : 2 * count], refs[2 * count]
    weights = softmax_parts(query[...], parts, biases)
    out[...] = sum(
        jnp.dot(weight.astype(BF16), part[1], preferred_element_type=F32)
        for weight, part in zip(weights, parts)
    ).astype(out.dtype)


def attend_back_kernel(count, query, out_grad, token_scale, *refs):
    parts, biases, refs = refs[:count], refs[count : 2 * count], refs[2 * count :]
    query_grad, part_grads, refs = refs[0], refs[1 : 1 + count], refs[1 + count :]
    queries, out_grads, refs = refs[0], refs[1], refs[2:]
    weights_all, scores_all = refs[:count], refs[count:]
    head = pl.program_id(0)
    rows = query.shape[0]
    here = pl.ds(pl.multiple_of(head * rows, rows), rows)
    scale = HD ** (-0.5)
    weights = softmax_parts(query[...], parts, biases)
    grad = out_grad[...]
    probs = [dot_rows(grad, part[1]) for part in parts]
    inner = sum(
        jnp.sum(weight * prob, axis=-1, keepdims=True) for weight, prob in zip(weights, probs)
    )
    scores = [
        (weight * (prob - inner)).astype(BF16) for weight, prob in zip(weights, probs)
    ]
    query_grad[...] = (
        sum(
            jnp.dot(score, part[0], preferred_element_type=F32)
            for score, part in zip(scores, parts)
        )
        * (token_scale[...] * scale)
    ).astype(query_grad.dtype)
    queries[here, :] = query[...]
    out_grads[here, :] = grad
    for i in range(count):
        weights_all[i][here, :] = weights[i].astype(BF16)
        scores_all[i][here, :] = scores[i]

    @pl.when(head == pl.num_programs(0) - 1)
    def _():
        for i in range(count):
            part_grads[i][0] = (dot_tokens(scores_all[i][...], queries[...]) * scale).astype(BF16)
            part_grads[i][1] = dot_tokens(weights_all[i][...], out_grads[...]).astype(BF16)


def whole_spec(shape):
    return pl.BlockSpec(shape, lambda i: (0,) * len(shape))


def attend(queries, parts, biases):
    rows, width = queries.shape
    span = sum(bias.shape[1] for bias in biases)
    head_spec = pl.BlockSpec((rows, HD), lambda i: (0, i))
    return pl.pallas_call(
        functools.partial(attend_kernel, len(parts)),
        grid=(width // HD,),
        in_specs=[head_spec] + [whole_spec(v.shape) for v in (*parts, *biases)],
        out_specs=head_spec,
        out_shape=jax.ShapeDtypeStruct(queries.shape, BF16),
        compiler_params=pltpu.CompilerParams(vmem_limit_bytes=48 * 1024 * 1024),
        cost_estimate=pl.CostEstimate(
            flops=4 * rows * width * span,
            bytes_accessed=4 * span * HD + 4 * rows * span + 4 * queries.size,
            transcendentals=rows * span * (width // HD),
        ),
    )(queries, *parts, *biases)


def attend_back(queries, out_grad, token_scale, parts, biases):
    rows, width = queries.shape
    heads = width // HD
    spans = [bias.shape[1] for bias in biases]
    head_spec = pl.BlockSpec((rows, HD), lambda i: (0, i))
    return pl.pallas_call(
        functools.partial(attend_back_kernel, len(parts)),
        grid=(heads,),
        in_specs=[head_spec, head_spec]
        + [whole_spec(v.shape) for v in (token_scale, *parts, *biases)],
        out_specs=[head_spec] + [whole_spec(part.shape) for part in parts],
        out_shape=[jax.ShapeDtypeStruct(queries.shape, BF16)]
        + [jax.ShapeDtypeStruct(part.shape, BF16) for part in parts],
        scratch_shapes=[pltpu.VMEM((heads * rows, HD), BF16)] * 2
        + [pltpu.VMEM((heads * rows, span), BF16) for span in spans] * 2,
        compiler_params=pltpu.CompilerParams(vmem_limit_bytes=56 * 1024 * 1024),
        cost_estimate=pl.CostEstimate(
            flops=10 * rows * width * sum(spans),
            bytes_accessed=8 * sum(spans) * HD + 4 * rows * sum(spans) + 6 * queries.size,
            transcendentals=rows * sum(spans) * heads,
        ),
    )(queries, out_grad, token_scale, *parts, *biases)


def geglu_kernel(tokens, cot, gate_weight, up_weight, down_weight, hidden, gate_up):
    step = pl.program_id(0)
    block = gate_weight.shape[1]
    gate = jnp.dot(tokens[...], gate_weight[...], preferred_element_type=F32)
    up = jnp.dot(tokens[...], up_weight[...], preferred_element_type=F32)
    hidden_grad = jnp.dot(cot[...], down_weight[...], preferred_element_type=F32)
    hidden_grad = hidden_grad.astype(BF16).astype(F32)
    root = 0.7978845608028654
    square = gate * gate
    bend = jnp.tanh(root * gate * (1.0 + 0.044715 * square))
    half = 0.5 * (1.0 + bend)
    gelu = gate * half
    slope = half + 0.5 * gate * (1.0 - bend * bend) * (root * (1.0 + 3 * 0.044715 * square))
    here = pl.ds(pl.multiple_of(step * block, block), block)
    hidden[:, here] = (gelu * up).astype(BF16)
    gate_up[:, here] = (hidden_grad * up * slope).astype(BF16)
    there = pl.ds(pl.multiple_of(hidden.shape[1] + step * block, block), block)
    gate_up[:, there] = (hidden_grad * gelu).astype(BF16)


def geglu(tokens, cot, weights):
    rows, width = tokens.shape
    units = weights.shape[1] // 3
    block = 512 if units % 512 == 0 else 128
    steps = units // block
    token_spec = whole_spec(tokens.shape)
    return pl.pallas_call(
        geglu_kernel,
        grid=(steps,),
        in_specs=[
            token_spec,
            token_spec,
            pl.BlockSpec((width, block), lambda i: (0, i)),
            pl.BlockSpec((width, block), lambda i: (0, steps + i)),
            pl.BlockSpec((width, block), lambda i: (0, 2 * steps + i)),
        ],
        out_specs=[whole_spec((rows, units)), whole_spec((rows, 2 * units))],
        out_shape=[
            jax.ShapeDtypeStruct((rows, units), BF16),
            jax.ShapeDtypeStruct((rows, 2 * units), BF16),
        ],
        compiler_params=pltpu.CompilerParams(vmem_limit_bytes=56 * 1024 * 1024),
        cost_estimate=pl.CostEstimate(
            flops=2 * rows * width * 3 * units,
            bytes_accessed=2 * weights.size + 4 * tokens.size + 6 * rows * units,
            transcendentals=rows * units,
        ),
    )(tokens, cot, weights, weights, weights)


def outer_kernel(count, *refs):
    out = refs[-1]
    first = 0
    for i in range(count):
        left, right = refs[2 * i], refs[2 * i + 1]
        columns = right.shape[1]
        tokens_first = left.shape[0] == right.shape[0]
        step = 512 if columns % 512 == 0 else columns
        for at in range(0, columns, step):
            out[:, first + at : first + at + step] = lax.dot_general(
                left[...],
                right[:, at : at + step],
                (((0 if tokens_first else 1,), (0,)), ((), ())),
                preferred_element_type=F32,
            ).astype(out.dtype)
        first += columns


def token_outer(*pairs):
    tokens, height = pairs[0][0].shape
    columns = sum(right.shape[1] for _, right in pairs)
    block = 256 if height % 256 == 0 else 128
    specs, operands = [], []
    for left, right in pairs:
        specs += [
            pl.BlockSpec((tokens, block), lambda i: (0, i))
            if left.shape[0] == tokens
            else pl.BlockSpec((block, tokens), lambda i: (i, 0)),
            pl.BlockSpec(right.shape, lambda i: (0, 0)),
        ]
        operands += [left, right]
    return pl.pallas_call(
        functools.partial(outer_kernel, len(pairs)),
        grid=(height // block,),
        in_specs=specs,
        out_specs=pl.BlockSpec((block, columns), lambda i: (i, 0)),
        out_shape=jax.ShapeDtypeStruct((height, columns), BF16),
        compiler_params=pltpu.CompilerParams(vmem_limit_bytes=40 * 1024 * 1024),
        cost_estimate=pl.CostEstimate(
            flops=2 * tokens * height * columns,
            bytes_accessed=2 * height * columns + 2 * tokens * (height * len(pairs) + columns),
            transcendentals=0,
        ),
    )(*operands)


def body(
    inputs,
    attn_gain,
    query_weight,
    keyval_weight,
    out_weight,
    ffn_gain,
    gate_weight,
    up_weight,
    down_weight,
    positions,
    cotangent,
):
    rows, width = inputs.shape
    own = attn_gain.shape[0]
    query_width = query_weight.shape[1]
    head_count = query_width // HD
    units = gate_weight.shape[1] // PLANES
    padded = -(-units // 128) * 128
    scale = HD ** (-0.5)
    plane = lax.axis_index(X)
    rank = lax.axis_index(R)
    half = lax.axis_index(M)
    gain_one = attn_gain.astype(F32)[:, None]
    gain_two = ffn_gain.astype(F32)[:, None]

    keyval_own = (
        lax.dynamic_slice_in_dim(keyval_weight, half * HD, HD, 1).astype(F32) * gain_one
    ).astype(BF16)
    query_own = (query_weight.astype(F32) * gain_one).astype(BF16)
    inputs_cut = cut_planes(inputs)
    tokens_in = inputs.astype(F32)
    scale_attn = rms_scale(tokens_in)

    def cut(weight):
        blocks = weight.reshape(own, PLANES, units)
        return jnp.pad(blocks, ((0, 0), (0, 0), (0, padded - units))).swapaxes(0, 1)

    ffn_own = jnp.concatenate(
        [
            cut((gate_weight.astype(F32) * gain_two).astype(BF16)),
            cut((up_weight.astype(F32) * gain_two).astype(BF16)),
            cut(down_weight.T),
        ],
        2,
    ).reshape(PLANES * own, 3 * padded)
    out_planes = lax.all_gather(out_weight.T, X, axis=0, tiled=True)
    both = gather_rows(jnp.concatenate([query_own, out_planes], 0))
    keyval_rows = spread(after(keyval_own, out_planes), R, RANKS)

    keyval = (
        reduce_planes(jnp.dot(inputs_cut, keyval_rows, preferred_element_type=F32)) * scale_attn
    ).astype(BF16)
    keyval_before = to_plane(keyval, 1)
    ranks = jnp.arange(RANKS, dtype=jnp.int32)
    ahead = (ranks >= rank)[:, None, None]
    ffn_own = lax.all_to_all(after(ffn_own, keyval_before), X, 0, 0, tiled=True)
    ffn = gather_rows(ffn_own)
    gate_up = ffn[:, : 2 * padded]
    down = ffn[:, 2 * padded :]
    part_rows = rows // PARTS

    def fetch(part):
        mine, before = (
            v[part * part_rows : (part + 1) * part_rows] for v in (keyval, keyval_before)
        )
        chosen = jnp.where(ahead, mine[None], before[None])
        sent = jnp.broadcast_to(chosen[None], (2, RANKS, part_rows, HD))
        met = lax.all_to_all(
            sent.reshape(2 * RANKS * part_rows, HD), (M,) + R, 0, 0, tiled=True
        )
        return met.reshape(2, RANKS * part_rows, HD)

    before_other = swap(keyval_before)
    first = half == 0
    last = jnp.where(
        first,
        jnp.stack([keyval_before, before_other]),
        jnp.stack([before_other, keyval_before]),
    )
    window = [fetch(part) for part in range(PARTS)]
    residual, cot = lax.optimization_barrier(
        (
            permute_features(after(inputs, keyval_before)),
            permute_features(after(cotangent, keyval_before)),
        )
    )
    both = after(both, window[0]).reshape(RANKS, (1 + PLANES) * own, query_width)
    query_rows, out_rows = lax.optimization_barrier(
        (
            both[:, :own].reshape(RANKS * own, query_width),
            both[:, own:].reshape(width, query_width),
        )
    )
    keyval_planes = gather_planes(after(keyval_rows, keyval_before))
    keyval_proj = jnp.concatenate(natural(keyval_planes.reshape(PLANES, RANKS * own, HD)), 0)
    queries_sum = reduce_planes(jnp.dot(inputs_cut, query_rows, preferred_element_type=F32))
    queries = after((queries_sum * scale_attn).astype(BF16), keyval_planes)

    block_own = plane * RANKS + rank
    offsets = jnp.arange(rows, dtype=jnp.int32)
    span = RANKS * rows
    pos_own = lax.dynamic_slice_in_dim(positions, plane * span, span, 0).reshape(RANKS, rows)
    pos_before = lax.dynamic_slice_in_dim(
        positions, jnp.maximum(plane - 1, 0) * span, span, 0
    ).reshape(RANKS, rows)
    pos_last = lax.dynamic_slice_in_dim(pos_before, rank, 1, 0)
    pos_window = jnp.where((ranks <= rank)[:, None], pos_own, pos_before)
    index_window = (
        (plane * RANKS + ranks - jnp.where(ranks <= rank, 0, RANKS)) * rows
    )[:, None] + offsets[None]
    index_last = (block_own - RANKS) * rows + offsets[None]

    def in_parts(window_values, last_values):
        cut_up = window_values.reshape(RANKS, PARTS, part_rows).swapaxes(0, 1)
        return jnp.concatenate([cut_up.reshape(-1), last_values.reshape(-1)])

    key_index = in_parts(index_window, index_last)
    pos_keys = in_parts(pos_window, pos_last)
    pos_query = lax.dynamic_slice_in_dim(positions, block_own * rows, rows, 0)
    query_index = block_own * rows + offsets
    allowed = (
        (key_index[None, :] >= 0)
        & (key_index[None, :] <= query_index[:, None])
        & (pos_query[:, None] - pos_keys[None, :] < WINDOW)
    )

    bias = jnp.where(allowed, 0.0, -1e30)
    part_span = RANKS * part_rows
    biases = [bias[:, i * part_span : (i + 1) * part_span] for i in range(PARTS)]
    biases.append(bias[:, PARTS * part_span :])
    attended = attend(queries, window + [last], biases)
    branch = sum_mp(jnp.einsum("te,de->td", attended, out_rows, preferred_element_type=F32))
    cot_all = gather_planes(after(cot, queries))
    middle = residual.astype(F32) + after(branch, cot_all)

    scale_ffn = rms_scale(middle)
    normed = (middle * scale_ffn).astype(BF16)
    normed_all = gather_planes(normed)
    hidden, gate_up_low = geglu(normed_all, cot_all, ffn)
    weighted_part = jnp.einsum("tf,ef->te", gate_up_low, gate_up, preferred_element_type=F32)
    weighted_low = rounded(reduce_planes(weighted_part))
    ffn_grad_part = token_outer(
        (normed_all, after(gate_up_low, weighted_part)), (cot_all, hidden)
    )
    ffn_grad_rows = lax.psum_scatter(ffn_grad_part, R, scatter_dimension=0, tiled=True)
    attended_all = gather_planes(after(attended, weighted_low))
    weighted = weighted_low.astype(F32) + after(swap(weighted_low), attended_all).astype(F32)

    middle_grad = cot.astype(F32) + norm_back(middle, scale_ffn, weighted)
    branch_low = middle_grad.astype(BF16)
    attended_grad = jnp.dot(branch_low, out_rows, preferred_element_type=F32).astype(BF16)
    query_scaled, *part_grads = attend_back(
        queries, attended_grad, scale_attn, window + [last], biases
    )
    branch_turned = branch_low.T.reshape(RANKS, PLANES, own, rows)
    branch_cut = cut_features(branch_turned.swapaxes(0, 1).reshape(PLANES, RANKS * own, rows))
    last_grad = part_grads.pop()
    part_grads[0], branch_cut = lax.optimization_barrier((part_grads[0], branch_cut))

    hidden = after(hidden, branch_cut)
    ffn_part = jnp.einsum("tf,ef->te", hidden, down, preferred_element_type=F32)
    ffn_low = rounded(reduce_planes(ffn_part))
    ffn_sum = ffn_low.astype(F32) + swap(ffn_low).astype(F32)
    activations = restore_features((middle + ffn_sum).astype(BF16))

    def send_back(grad):
        returned = lax.all_to_all(
            grad.reshape(2 * RANKS * part_rows, HD), (M,) + R, 0, 0, tiled=True
        )
        return returned.reshape(2, RANKS, part_rows, HD)

    returned = [send_back(grad) for grad in part_grads]
    returned[0] = after(returned[0], ffn_low)
    query_all = gather_planes(after(query_scaled, returned[0]))
    attn_grad_part = after(
        token_outer((inputs_cut, query_all), (branch_cut, attended_all)), ffn_grad_rows
    )
    returned[-1] = after(returned[-1], attn_grad_part)
    last_other = swap(jnp.where(first, last_grad[1], last_grad[0]))
    last_mine = jnp.where(first, last_grad[0], last_grad[1])
    own_sum = jnp.concatenate(
        [jnp.sum(jnp.where(ahead, part, 0).astype(F32), (0, 1)) for part in returned], 0
    )
    before_sum = (
        jnp.concatenate(
            [jnp.sum(jnp.where(ahead, 0, part).astype(F32), (0, 1)) for part in returned], 0
        )
        + last_mine.astype(F32)
        + last_other.astype(F32)
    )
    keyval_grad = own_sum + to_plane(rounded(before_sum), -1).astype(F32)
    keyval_scaled = (keyval_grad.astype(BF16).astype(F32) * scale_attn).astype(BF16)


    input_part = jnp.einsum("te,de->td", query_all, query_rows, preferred_element_type=F32)
    weighted_one = sum_mp(
        join_planes(input_part.astype(BF16)).astype(F32)
        + jnp.einsum("tc,dc->td", keyval_scaled, keyval_proj, preferred_element_type=F32)
    )
    input_grad = (
        restore_features(after(middle_grad, keyval_grad))
        + weighted_one
        - tokens_in
        * scale_attn**2
        * jnp.mean(weighted_one * tokens_in, axis=-1, keepdims=True)
    )

    def to_owner(part):
        met = lax.all_to_all(part, R, 0, 0, tiled=True)
        return jnp.sum(met.reshape(RANKS, own, part.shape[1]).astype(F32), 0)

    attn_base = lax.psum_scatter(
        attn_grad_part, R, scatter_dimension=0, tiled=True
    ).astype(F32)
    query_base = attn_base[:, :query_width]
    out_weight_grad = attn_base[:, query_width:].T
    ffn_grad_own = jnp.stack(
        exchange_planes(ffn_grad_rows.reshape(PLANES, own, 3 * padded)), 0
    )
    keyval_grad_part = token_outer((inputs_cut, gather_planes(keyval_scaled)))
    keyval_mine = to_owner(keyval_grad_part)
    keyval_other = swap(keyval_mine)
    keyval_base = jnp.concatenate(
        [
            jnp.where(first, keyval_mine, keyval_other),
            jnp.where(first, keyval_other, keyval_mine),
        ],
        1,
    )

    def join(first_column):
        piece = ffn_grad_own[:, :, first_column : first_column + units]
        return piece.swapaxes(0, 1).reshape(own, PLANES * units).astype(F32)

    gate_base = join(0)
    up_base = join(padded)
    down_weight_grad = join(2 * padded).T

    def gain_sum(values):
        part = jnp.sum(values, axis=1)[None]
        return (part + swap(part))[0]

    ffn_gain_grad = gain_sum(
        gate_weight.astype(F32) * gate_base + up_weight.astype(F32) * up_base
    )
    attn_gain_grad = gain_sum(query_weight.astype(F32) * query_base) + jnp.sum(
        keyval_weight.astype(F32) * keyval_base, axis=1
    )

    return (
        activations,
        input_grad,
        attn_gain_grad,
        query_base * gain_one,
        keyval_base * gain_one,
        out_weight_grad,
        ffn_gain_grad,
        gate_base * gain_two,
        up_base * gain_two,
        down_weight_grad,
    )


def solution(mesh):
    axes = (X,) + R
    cut = Mesh(mesh.devices.reshape((PLANES,) + RANK_SIZES + (2,)), axes + (M,))
    return jax.shard_map(
        body,
        mesh=cut,
        in_specs=(
            P(axes, None),
            P(axes),
            P(axes, M),
            P(axes, None),
            P(M, axes),
            P(axes),
            P(axes, M),
            P(axes, M),
            P(M, axes),
            P(),
            P(axes, None),
        ),
        out_specs=(
            P(axes, None),
            P(axes, None),
            P(axes),
            P(axes, M),
            P(axes, None),
            P(M, axes),
            P(axes),
            P(axes, M),
            P(axes, M),
            P(M, axes),
        ),
        check_vma=False,
    )
```

```python
import functools

import jax
import jax.numpy as jnp
from jax import lax
from jax.experimental import pallas as pl
from jax.experimental.pallas import tpu as pltpu
from jax.sharding import Mesh, PartitionSpec as P

HD = 256
WINDOW = 2048
EPS = 1e-06

PLANES = 4
RANK_SIZES = (2, 4, 2)
RANKS = 16
CHIPS = 8
X = "x"
R = ("yl", "z", "c")
CHIP = ("yl", "z")
CORE = "c"
M = "mp"

F32 = jnp.float32
BF16 = jnp.bfloat16


def after(value, *earlier):
    return lax.optimization_barrier((value,) + earlier)[0]


def rms_scale(values):
    return lax.rsqrt(jnp.mean(values * values, axis=-1, keepdims=True) + EPS)


def norm_back(values, scale_rows, weighted):
    return scale_rows * weighted - values * scale_rows**3 * jnp.mean(
        weighted * values, axis=-1, keepdims=True
    )


def to_plane(block, shift):
    return lax.ppermute(block, X, [(i, (i + shift) % PLANES) for i in range(PLANES)])


def swap(block):
    return lax.ppermute(block, M, [(0, 1), (1, 0)])


def swap_cores(block):
    return lax.ppermute(block, CORE, [(0, 1), (1, 0)])


def rounded(values):
    return lax.reduce_precision(values, 8, 7).astype(BF16)


def sum_mp(part):
    low = rounded(part)
    return low.astype(F32) + swap(low).astype(F32)


def gather_planes(block):
    half = block.shape[0] // 2
    after = to_plane(block, -1)
    before = to_plane(block, 1)
    far_top = to_plane(before[:half], 1)
    far_low = to_plane(after[half:], -1)
    return jnp.concatenate([block, after, far_top, far_low, before], 0)


def collect_planes(block):
    return [block, to_plane(block, 3), to_plane(block, 2), to_plane(block, 1)]


def reduce_far(part):
    rows = part.shape[0] // PLANES
    half = rows // 2
    own, after_one, far, before_one = (
        part[i * rows : (i + 1) * rows].astype(F32) for i in range(PLANES)
    )
    far = rounded(far)
    top = to_plane(far[:half], 1).astype(F32)
    low = to_plane(far[half:], -1).astype(F32)
    after_one = jnp.concatenate([after_one[:half] + top, after_one[half:]], 0)
    before_one = jnp.concatenate([before_one[:half], before_one[half:] + low], 0)
    return own, rounded(after_one), rounded(before_one)


def reduce_near(own, after_one, before_one):
    return own + to_plane(before_one, -1).astype(F32) + to_plane(after_one, 1).astype(F32)


def reduce_planes(part):
    return reduce_near(*reduce_far(part))


def pick(blocks, index):
    return lax.dynamic_index_in_dim(blocks, lax.rem(index + PLANES, PLANES), 0, keepdims=False)


def natural(blocks):
    plane = lax.axis_index(X)
    return [pick(blocks, p - plane) for p in range(PLANES)]


def send_planes(blocks):
    plane = lax.axis_index(X)
    return [pick(blocks, plane)] + [
        to_plane(pick(blocks, plane + k), k) for k in range(1, PLANES)
    ]


def exchange_planes(blocks):
    plane = lax.axis_index(X)
    got = jnp.stack(send_planes(blocks))
    return [pick(got, plane - p) for p in range(PLANES)]


def cut_planes(values):
    rows, width = values.shape
    got = send_planes(values.reshape(rows, PLANES, width // PLANES).swapaxes(0, 1))
    return jnp.concatenate([got[0], got[3], got[2], got[1]], 0)


def cut_features(blocks):
    got = send_planes(blocks)
    return [got[0], got[3], got[2], got[1]]


def join_planes(blocks):
    got = jnp.stack([blocks[0]] + [to_plane(blocks[k], k) for k in range(1, PLANES)])
    plane = lax.axis_index(X)
    return jnp.concatenate([pick(got, plane - p) for p in range(PLANES)], 1)


def permute_features(values):
    rows, width = values.shape
    cut = values.reshape(rows, PLANES, RANKS, width // (PLANES * RANKS))
    return cut.swapaxes(1, 2).reshape(rows, width)


def restore_features(values):
    rows, width = values.shape
    cut = values.reshape(rows, RANKS, PLANES, width // (PLANES * RANKS))
    return cut.swapaxes(1, 2).reshape(rows, width)


def spread(block, axes, size):
    rows, columns = block.shape
    copies = jnp.broadcast_to(block[None], (size, rows, columns)).reshape(size * rows, columns)
    return lax.all_to_all(copies, axes, 0, 0, tiled=True)


def gather_rows(block):
    return lax.all_gather(block, R, axis=0, tiled=True)


def dot_rows(left, right):
    return lax.dot_general(left, right, (((1,), (1,)), ((), ())), preferred_element_type=F32)


def dot_tokens(left, right):
    return lax.dot_general(left, right, (((0,), (0,)), ((), ())), preferred_element_type=F32)


def softmax_parts(query, parts, biases):
    scale = HD ** (-0.5)
    scores = [dot_rows(query, part[0]) * scale + bias[...] for part, bias in zip(parts, biases)]
    top = functools.reduce(
        jnp.maximum, [jnp.max(score, axis=-1, keepdims=True) for score in scores]
    )
    scores = [jnp.exp(score - top) for score in scores]
    inverse = 1.0 / sum(jnp.sum(score, axis=-1, keepdims=True) for score in scores)
    return [score * inverse for score in scores]


def attend_kernel(count, query, *refs):
    parts, biases, out = refs[:count], refs[count : 2 * count], refs[2 * count]
    weights = softmax_parts(query[...], parts, biases)
    out[...] = sum(
        jnp.dot(weight.astype(BF16), part[1], preferred_element_type=F32)
        for weight, part in zip(weights, parts)
    ).astype(out.dtype)


def attend_back_kernel(
    core, query, out_grad, attended, token_scale, *refs
):
    parts, biases, refs = refs[:3], refs[3:6], refs[6:]
    both, window_grad, last_grad, refs = refs[0], refs[1], refs[2], refs[3:]
    queries, out_grads, refs = refs[0], refs[1], refs[2:]
    weights_all, scores_all = refs[:3], refs[3:]
    head = pl.program_id(0)
    heads = pl.num_programs(0)
    rows = query.shape[0]
    here = pl.ds(pl.multiple_of(head * rows, rows), rows)
    scale = HD ** (-0.5)
    weights = softmax_parts(query[...], parts, biases)
    grad = out_grad[...]
    probs = [dot_rows(grad, part[1]) for part in parts]
    inner = sum(
        jnp.sum(weight * prob, axis=-1, keepdims=True) for weight, prob in zip(weights, probs)
    )
    scores = [
        (weight * (prob - inner)).astype(BF16) for weight, prob in zip(weights, probs)
    ]
    both[:, pl.ds(pl.multiple_of(head * HD, HD), HD)] = (
        sum(
            jnp.dot(score, part[0], preferred_element_type=F32)
            for score, part in zip(scores, parts)
        )
        * (token_scale[...] * scale)
    ).astype(both.dtype)
    both[:, pl.ds(pl.multiple_of((heads + head) * HD, HD), HD)] = attended[...]
    queries[here, :] = query[...]
    out_grads[here, :] = grad
    for i in range(3):
        weights_all[i][here, :] = weights[i].astype(BF16)
        scores_all[i][here, :] = scores[i]

    @pl.when(head == heads - 1)
    def _():
        for i in range(3):
            key = (dot_tokens(scores_all[i][...], queries[...]) * scale).astype(BF16)
            value = dot_tokens(weights_all[i][...], out_grads[...]).astype(BF16)
            if i == 2:
                last_grad[0] = key
                last_grad[1] = value
            else:
                which = core[0] if i == 0 else 1 - core[0]
                shape = (CHIPS, 1, rows, HD)
                window_grad[0, :, pl.ds(which, 1)] = key.reshape(shape)
                window_grad[1, :, pl.ds(which, 1)] = value.reshape(shape)


def whole_spec(shape):
    return pl.BlockSpec(shape, lambda i: (0,) * len(shape))


def attend(queries, parts, biases):
    rows, width = queries.shape
    span = sum(bias.shape[1] for bias in biases)
    head_spec = pl.BlockSpec((rows, HD), lambda i: (0, i))
    return pl.pallas_call(
        functools.partial(attend_kernel, len(parts)),
        grid=(width // HD,),
        in_specs=[head_spec] + [whole_spec(v.shape) for v in (*parts, *biases)],
        out_specs=head_spec,
        out_shape=jax.ShapeDtypeStruct(queries.shape, BF16),
        compiler_params=pltpu.CompilerParams(vmem_limit_bytes=48 * 1024 * 1024),
        cost_estimate=pl.CostEstimate(
            flops=4 * rows * width * span,
            bytes_accessed=4 * span * HD + 4 * rows * span + 4 * queries.size,
            transcendentals=rows * span * (width // HD),
        ),
    )(queries, *parts, *biases)


def attend_back(core, queries, out_grad, attended, token_scale, parts, biases):
    rows, width = queries.shape
    heads = width // HD
    spans = [bias.shape[1] for bias in biases]
    head_spec = pl.BlockSpec((rows, HD), lambda i: (0, i))
    shapes = [(rows, 2 * width), (2, CHIPS, 2, rows, HD), parts[-1].shape]
    return pl.pallas_call(
        attend_back_kernel,
        grid=(heads,),
        in_specs=[pl.BlockSpec(memory_space=pltpu.SMEM), head_spec, head_spec, head_spec]
        + [whole_spec(v.shape) for v in (token_scale, *parts, *biases)],
        out_specs=[whole_spec(shape) for shape in shapes],
        out_shape=[jax.ShapeDtypeStruct(shape, BF16) for shape in shapes],
        scratch_shapes=[pltpu.VMEM((heads * rows, HD), BF16)] * 2
        + [pltpu.VMEM((heads * rows, span), BF16) for span in spans] * 2,
        compiler_params=pltpu.CompilerParams(vmem_limit_bytes=56 * 1024 * 1024),
        cost_estimate=pl.CostEstimate(
            flops=10 * rows * width * sum(spans),
            bytes_accessed=8 * sum(spans) * HD + 4 * rows * sum(spans) + 6 * queries.size,
            transcendentals=rows * sum(spans) * heads,
        ),
    )(core.reshape(1), queries, out_grad, attended, token_scale, *parts, *biases)


def geglu_kernel(tokens, cot, gate_weight, up_weight, down_weight, hidden, gate_up):
    step = pl.program_id(0)
    block = gate_weight.shape[1]
    gate = jnp.dot(tokens[...], gate_weight[...], preferred_element_type=F32)
    up = jnp.dot(tokens[...], up_weight[...], preferred_element_type=F32)
    hidden_grad = jnp.dot(cot[...], down_weight[...], preferred_element_type=F32)
    hidden_grad = hidden_grad.astype(BF16).astype(F32)
    root = 0.7978845608028654
    square = gate * gate
    bend = jnp.tanh(root * gate * (1.0 + 0.044715 * square))
    half = 0.5 * (1.0 + bend)
    gelu = gate * half
    slope = half + 0.5 * gate * (1.0 - bend * bend) * (root * (1.0 + 3 * 0.044715 * square))
    here = pl.ds(pl.multiple_of(step * block, block), block)
    hidden[:, here] = (gelu * up).astype(BF16)
    gate_up[:, here] = (hidden_grad * up * slope).astype(BF16)
    there = pl.ds(pl.multiple_of(hidden.shape[1] + step * block, block), block)
    gate_up[:, there] = (hidden_grad * gelu).astype(BF16)


def geglu(tokens, cot, weights):
    rows, width = tokens.shape
    units = weights.shape[1] // 3
    block = 256 if units % 256 == 0 else 128
    steps = units // block
    token_spec = pl.BlockSpec(tokens.shape, lambda i: (0, 0), pipeline_mode=pl.Buffered(1))
    return pl.pallas_call(
        geglu_kernel,
        grid=(steps,),
        in_specs=[
            token_spec,
            token_spec,
            pl.BlockSpec((width, block), lambda i: (0, i)),
            pl.BlockSpec((width, block), lambda i: (0, steps + i)),
            pl.BlockSpec((width, block), lambda i: (0, 2 * steps + i)),
        ],
        out_specs=[whole_spec((rows, units)), whole_spec((rows, 2 * units))],
        out_shape=[
            jax.ShapeDtypeStruct((rows, units), BF16),
            jax.ShapeDtypeStruct((rows, 2 * units), BF16),
        ],
        compiler_params=pltpu.CompilerParams(vmem_limit_bytes=56 * 1024 * 1024),
        cost_estimate=pl.CostEstimate(
            flops=2 * rows * width * 3 * units,
            bytes_accessed=2 * weights.size + 4 * tokens.size + 6 * rows * units,
            transcendentals=rows * units,
        ),
    )(tokens, cot, weights, weights, weights)


def outer_kernel(count, *refs):
    out = refs[-1]
    first = 0
    for i in range(count):
        left, right = refs[2 * i], refs[2 * i + 1]
        columns = right.shape[1]
        tokens_first = left.shape[0] == right.shape[0]
        step = 512 if columns % 512 == 0 else columns
        for at in range(0, columns, step):
            out[:, first + at : first + at + step] = lax.dot_general(
                left[...],
                right[:, at : at + step],
                (((0 if tokens_first else 1,), (0,)), ((), ())),
                preferred_element_type=F32,
            ).astype(out.dtype)
        first += columns


def token_outer(*pairs):
    tokens, height = pairs[0][0].shape
    columns = sum(right.shape[1] for _, right in pairs)
    block = next(size for size in (512, 640, 256, 128) if height % size == 0)
    specs, operands = [], []
    for left, right in pairs:
        specs += [
            pl.BlockSpec((tokens, block), lambda i: (0, i))
            if left.shape[0] == tokens
            else pl.BlockSpec((block, tokens), lambda i: (i, 0)),
            pl.BlockSpec(right.shape, lambda i: (0, 0)),
        ]
        operands += [left, right]
    return pl.pallas_call(
        functools.partial(outer_kernel, len(pairs)),
        grid=(height // block,),
        in_specs=specs,
        out_specs=pl.BlockSpec((block, columns), lambda i: (i, 0)),
        out_shape=jax.ShapeDtypeStruct((height, columns), BF16),
        compiler_params=pltpu.CompilerParams(vmem_limit_bytes=40 * 1024 * 1024),
        cost_estimate=pl.CostEstimate(
            flops=2 * tokens * height * columns,
            bytes_accessed=2 * height * columns + 2 * tokens * (height * len(pairs) + columns),
            transcendentals=0,
        ),
    )(*operands)


def attn_outer_kernel(*refs):
    inputs, cuts, boths = refs[0], refs[1:5], refs[5:9]
    out = refs[9]
    rows, width = boths[0].shape[0], boths[0].shape[1] // 2
    out[:, :width] = sum(
        dot_tokens(inputs[k * rows : (k + 1) * rows, :], boths[k][:, :width])
        for k in range(PLANES)
    ).astype(out.dtype)
    out[:, width:] = sum(
        jnp.dot(cuts[k][...], boths[k][:, width:], preferred_element_type=F32)
        for k in range(PLANES)
    ).astype(out.dtype)


def attn_outer(inputs, cuts, boths):
    height, columns = inputs.shape[1], boths[0].shape[1]
    rows = boths[0].shape[0]
    block = 128
    return pl.pallas_call(
        attn_outer_kernel,
        grid=(height // block,),
        in_specs=[pl.BlockSpec((inputs.shape[0], block), lambda i: (0, i))]
        + [pl.BlockSpec((block, rows), lambda i: (i, 0))] * PLANES
        + [whole_spec(boths[0].shape)] * PLANES,
        out_specs=pl.BlockSpec((block, columns), lambda i: (i, 0)),
        out_shape=jax.ShapeDtypeStruct((height, columns), BF16),
        compiler_params=pltpu.CompilerParams(vmem_limit_bytes=40 * 1024 * 1024),
        cost_estimate=pl.CostEstimate(
            flops=2 * PLANES * rows * height * columns,
            bytes_accessed=2 * (height + PLANES * rows) * columns + 4 * inputs.size,
            transcendentals=0,
        ),
    )(inputs, *cuts, *boths)


def input_back_kernel(*refs):
    boths, keyvals, query_rows, keyval_rows = refs[:4], refs[4:8], refs[8], refs[9]
    keyval_out, outs = refs[10], refs[11:]
    rows, width = boths[0].shape[0], boths[0].shape[1] // 2
    for k in range(PLANES):
        keyval = (
            keyvals[k][:rows].astype(F32) + keyvals[(k + 1) % PLANES][rows:].astype(F32)
        ).astype(BF16)
        keyval_out[k * rows : (k + 1) * rows] = keyval
        outs[k][...] = (
            dot_rows(boths[k][:, :width], query_rows[...]) + dot_rows(keyval, keyval_rows[...])
        ).astype(outs[k].dtype)


def input_back(boths, keyvals, query_rows, keyval_rows):
    rows = boths[0].shape[0]
    height = query_rows.shape[0]
    shapes = [(PLANES * rows, HD)] + [(rows, height)] * PLANES
    operands = (*boths, *keyvals, query_rows, keyval_rows)
    return pl.pallas_call(
        input_back_kernel,
        grid=(1,),
        in_specs=[whole_spec(v.shape) for v in operands],
        out_specs=[whole_spec(shape) for shape in shapes],
        out_shape=[jax.ShapeDtypeStruct(shape, BF16) for shape in shapes],
        compiler_params=pltpu.CompilerParams(vmem_limit_bytes=40 * 1024 * 1024),
        cost_estimate=pl.CostEstimate(
            flops=2 * PLANES * rows * height * query_rows.shape[1],
            bytes_accessed=2 * sum(v.size for v in operands) + 2 * PLANES * rows * height,
            transcendentals=0,
        ),
    )(*operands)


def join_kernel(padded, gate_weight, up_weight, gain, *refs):
    pieces, outs, gain_out = refs[:PLANES], refs[PLANES : PLANES + 3], refs[PLANES + 3]
    units = gate_weight.shape[1] // PLANES
    total = jnp.zeros((gate_weight.shape[0], 1), F32)
    for p in range(PLANES):
        columns = slice(p * units, (p + 1) * units)
        gate = pieces[p][:, :units].astype(F32)
        up = pieces[p][:, padded : padded + units].astype(F32)
        total += jnp.sum(
            gate_weight[:, columns].astype(F32) * gate + up_weight[:, columns].astype(F32) * up,
            axis=1,
            keepdims=True,
        )
        outs[0][:, columns] = gate * gain[...]
        outs[1][:, columns] = up * gain[...]
        outs[2][:, columns] = pieces[p][:, 2 * padded : 2 * padded + units].astype(F32)
    gain_out[...] = total


def join(pieces, gate_weight, up_weight, gain):
    shape = gate_weight.shape
    padded = pieces[0].shape[1] // 3
    operands = (gate_weight, up_weight, gain, *pieces)
    shapes = [shape] * 3 + [(shape[0], 1)]
    return pl.pallas_call(
        functools.partial(join_kernel, padded),
        grid=(1,),
        in_specs=[whole_spec(v.shape) for v in operands],
        out_specs=[whole_spec(one) for one in shapes],
        out_shape=[jax.ShapeDtypeStruct(one, F32) for one in shapes],
        compiler_params=pltpu.CompilerParams(vmem_limit_bytes=40 * 1024 * 1024),
        cost_estimate=pl.CostEstimate(
            flops=10 * gate_weight.size,
            bytes_accessed=24 * gate_weight.size,
            transcendentals=0,
        ),
    )(*operands)


def body(
    inputs,
    attn_gain,
    query_weight,
    keyval_weight,
    out_weight,
    ffn_gain,
    gate_weight,
    up_weight,
    down_weight,
    positions,
    cotangent,
):
    rows, width = inputs.shape
    own = attn_gain.shape[0]
    query_width = query_weight.shape[1]
    head_count = query_width // HD
    units = gate_weight.shape[1] // PLANES
    padded = -(-units // 128) * 128
    scale = HD ** (-0.5)
    plane = lax.axis_index(X)
    rank = lax.axis_index(R)
    half = lax.axis_index(M)
    core = lax.axis_index(CORE)
    chip = lax.axis_index(CHIP)
    chips = jnp.arange(CHIPS, dtype=jnp.int32)
    ahead = (chips >= chip)[:, None, None]
    at_home = (chips == chip)[:, None, None]
    gain_one = attn_gain.astype(F32)[:, None]
    gain_two = ffn_gain.astype(F32)[:, None]

    keyval_own = (
        lax.dynamic_slice_in_dim(keyval_weight, half * HD, HD, 1).astype(F32) * gain_one
    ).astype(BF16)
    query_own = (query_weight.astype(F32) * gain_one).astype(BF16)
    inputs_cut = cut_planes(inputs)
    tokens_in = inputs.astype(F32)
    scale_attn = rms_scale(tokens_in)
    scale_before = to_plane(scale_attn.reshape(1, rows), 1).reshape(rows, 1)

    def cut(weight):
        blocks = weight.reshape(own, PLANES, units)
        return jnp.pad(blocks, ((0, 0), (0, 0), (0, padded - units))).swapaxes(0, 1)

    ffn_own = jnp.concatenate(
        [
            cut((gate_weight.astype(F32) * gain_two).astype(BF16)),
            cut((up_weight.astype(F32) * gain_two).astype(BF16)),
            cut(down_weight.T),
        ],
        2,
    ).reshape(PLANES * own, 3 * padded)
    out_planes = lax.all_gather(out_weight.T, X, axis=0, tiled=True)
    both = gather_rows(jnp.concatenate([query_own, out_planes], 0))
    ffn_own = lax.all_to_all(after(ffn_own, out_planes), X, 0, 0, tiled=True)
    ffn = gather_rows(ffn_own)
    keyval_rows = spread(after(keyval_own, ffn_own), R, RANKS)

    ranks = jnp.arange(RANKS, dtype=jnp.int32)
    block_own = plane * RANKS + rank
    offsets = jnp.arange(rows, dtype=jnp.int32)
    span = RANKS * rows
    pos_own = lax.dynamic_slice_in_dim(positions, plane * span, span, 0).reshape(RANKS, rows)
    pos_before = lax.dynamic_slice_in_dim(
        positions, jnp.maximum(plane - 1, 0) * span, span, 0
    ).reshape(RANKS, rows)
    pos_last = lax.dynamic_slice_in_dim(pos_before, rank, 1, 0)
    def in_parts(own_values, before_values, last_values):
        chosen = jnp.where((ranks <= rank)[:, None], own_values, before_values)
        cores = chosen.reshape(CHIPS, 2, rows)
        parts = [
            lax.dynamic_index_in_dim(cores, index, 1, keepdims=False).reshape(-1)
            for index in (core, 1 - core)
        ]
        return jnp.concatenate(parts + [last_values.reshape(-1)])

    index_own = ((plane * RANKS + ranks) * rows)[:, None] + offsets[None]
    key_index = in_parts(
        index_own, index_own - span, (block_own - RANKS) * rows + offsets
    )
    pos_keys = in_parts(pos_own, pos_before, pos_last)
    pos_query = lax.dynamic_slice_in_dim(positions, block_own * rows, rows, 0)
    query_index = block_own * rows + offsets
    allowed = (
        (key_index[None, :] >= 0)
        & (key_index[None, :] <= query_index[:, None])
        & (pos_query[:, None] - pos_keys[None, :] < WINDOW)
    )

    bias = jnp.where(allowed, 0.0, -1e30)
    part_span = CHIPS * rows
    biases = [
        bias[:, :part_span],
        bias[:, part_span : 2 * part_span],
        bias[:, 2 * part_span :],
    ]
    residual, cot = lax.optimization_barrier(
        (
            permute_features(after(inputs, ffn_own)),
            permute_features(after(cotangent, ffn_own)),
        )
    )

    keyval = (
        reduce_planes(
            jnp.dot(
                inputs_cut,
                keyval_rows,
                preferred_element_type=F32,
            )
        )
        * scale_attn
    ).astype(BF16)
    keyval_before = to_plane(keyval, 1)
    before_other = to_plane(swap(keyval), 1)
    down = ffn[:, 2 * padded :]

    both = both.reshape(RANKS, (1 + PLANES) * own, query_width)
    query_rows = lax.optimization_barrier(both[:, :own].reshape(RANKS * own, query_width))
    out_rows = both[:, own:].reshape(width, query_width)
    queries_part = jnp.dot(after(inputs_cut, before_other), query_rows, preferred_element_type=F32)
    queries_sum = reduce_planes(queries_part)
    first = half == 0
    last = jnp.where(
        first,
        jnp.stack([keyval_before, before_other]),
        jnp.stack([before_other, keyval_before]),
    )
    chosen = jnp.where(ahead, keyval[None], keyval_before[None])
    sent = jnp.broadcast_to(chosen[None], (2, CHIPS, rows, HD))
    met = lax.all_to_all(
        sent.reshape(2 * CHIPS * rows, HD), (M,) + CHIP, 0, 0, tiled=True
    ).reshape(2, CHIPS, rows, HD)
    met_lent = jnp.where(at_home & (core == 1), last[:, None], met)
    met_other = swap_cores(after(met_lent, queries_sum))
    window = [v.reshape(2, CHIPS * rows, HD) for v in (met, met_other)]
    queries, out_rows = lax.optimization_barrier(
        ((queries_sum * scale_attn).astype(BF16), out_rows)
    )

    attended = attend(queries, window + [last], biases)
    branch_part = jnp.einsum("te,de->td", attended, out_rows, preferred_element_type=F32)
    branch = sum_mp(branch_part)
    cot_all = gather_planes(after(cot, queries))
    middle = residual.astype(F32) + after(branch, cot_all)

    scale_ffn = rms_scale(middle)
    normed = (middle * scale_ffn).astype(BF16)
    normed_all = gather_planes(normed)
    hidden, gate_up_low = geglu(normed_all, cot_all, ffn)
    ffn_grad_part = token_outer((normed_all, gate_up_low), (cot_all, hidden))
    ffn_grad_rows = lax.psum_scatter(ffn_grad_part, R, scatter_dimension=0, tiled=True)
    gate_up_low = after(gate_up_low, ffn_grad_part)
    weighted_part = jnp.einsum(
        "tf,ef->te", gate_up_low, ffn[:, : 2 * padded], preferred_element_type=F32
    ).astype(BF16)
    weighted_low = rounded(reduce_planes(weighted_part))
    weighted = weighted_low.astype(F32) + swap(weighted_low).astype(F32)

    middle_grad = cot.astype(F32) + norm_back(middle, scale_ffn, weighted)
    branch_low = middle_grad.astype(BF16)
    attended_grad = jnp.dot(branch_low, out_rows, preferred_element_type=F32).astype(BF16)
    query_both, window_grad, last_grad = attend_back(
        core, queries, attended_grad, attended, scale_attn, window + [last], biases
    )
    gathered = collect_planes(query_both)
    branch_late = after(branch_low, *gathered)
    branch_turned = branch_late.T.reshape(RANKS, PLANES, own, rows)
    branch_cut = cut_features(branch_turned.swapaxes(0, 1).reshape(PLANES, RANKS * own, rows))

    ffn_part = jnp.einsum(
        "tf,ef->te", after(hidden, *branch_cut), down, preferred_element_type=F32
    )
    ffn_low = rounded(reduce_planes(ffn_part))

    returned = lax.all_to_all(
        window_grad.reshape(2 * RANKS * rows, HD), (M,) + R, 0, 0, tiled=True
    ).reshape(2, RANKS, rows, HD)
    last_other = swap(jnp.where(first, last_grad[1], last_grad[0]))
    last_mine = jnp.where(first, last_grad[0], last_grad[1])
    own_plane = (ranks >= rank)[:, None, None]
    own_sum = jnp.sum(jnp.where(own_plane, returned, 0).astype(F32), (0, 1))
    before_sum = (
        jnp.sum(jnp.where(own_plane, 0, returned).astype(F32), (0, 1))
        + last_mine.astype(F32)
        + last_other.astype(F32)
    )

    keyval_pieces = collect_planes(
        rounded(jnp.concatenate([own_sum * scale_attn, before_sum * scale_before], 0))
    )
    attn_grad_part = attn_outer(inputs_cut, branch_cut, gathered)
    attn_width = attn_grad_part.shape[1]
    attn_cores = attn_grad_part.reshape(CHIPS, 2, own, attn_width)
    attn_lent = swap_cores(lax.dynamic_index_in_dim(attn_cores, 1 - core, 1, keepdims=False))
    attn_kept = lax.dynamic_index_in_dim(attn_cores, core, 1, keepdims=False)
    attn_chip = rounded(attn_kept.astype(F32) + attn_lent.astype(F32))
    attn_met = lax.all_to_all(
        attn_chip.reshape(CHIPS * own, attn_width), CHIP, 0, 0, tiled=True
    )
    keyval_all, *input_parts = input_back(gathered, keyval_pieces, query_rows, keyval_rows)
    ffn_grad_rows, middle_late, ffn_low, attn_met, *input_parts = lax.optimization_barrier(
        (ffn_grad_rows, middle_grad, ffn_low, attn_met, *input_parts)
    )
    weighted_low = rounded(join_planes(input_parts).astype(F32))
    ffn_grad_rows = after(ffn_grad_rows, weighted_low)
    attn_base = jnp.sum(attn_met.reshape(CHIPS, own, attn_width).astype(F32), 0)
    query_base = attn_base[:, :query_width]
    out_weight_grad = attn_base[:, query_width : 2 * query_width].T
    keyval_met = lax.all_to_all(
        after(token_outer((inputs_cut, keyval_all)), attn_met), R, 0, 0, tiled=True
    )
    keyval_mine = jnp.sum(keyval_met.reshape(RANKS, own, HD).astype(F32), 0)
    keyval_other = swap(keyval_mine)
    keyval_base = jnp.concatenate(
        [
            jnp.where(first, keyval_mine, keyval_other),
            jnp.where(first, keyval_other, keyval_mine),
        ],
        1,
    )

    weighted_one = weighted_low.astype(F32) + swap(weighted_low).astype(F32)
    input_grad = (
        restore_features(middle_late)
        + weighted_one
        - tokens_in
        * scale_attn**2
        * jnp.mean(weighted_one * tokens_in, axis=-1, keepdims=True)
    )

    ffn_sum = ffn_low.astype(F32) + swap(ffn_low).astype(F32)
    activations = restore_features((middle + ffn_sum).astype(BF16))
    ffn_grad_own = exchange_planes(ffn_grad_rows.reshape(PLANES, own, 3 * padded))
    gate_weight_grad, up_weight_grad, down_rows, ffn_gain_part = join(
        ffn_grad_own, gate_weight, up_weight, gain_two
    )

    def gain_sum(part):
        part = part.reshape(1, own)
        return (part + swap(part))[0]

    ffn_gain_grad = gain_sum(ffn_gain_part)
    attn_gain_grad = gain_sum(
        jnp.sum(query_weight.astype(F32) * query_base, axis=1)
    ) + jnp.sum(keyval_weight.astype(F32) * keyval_base, axis=1)

    return (
        activations,
        input_grad,
        attn_gain_grad,
        query_base * gain_one,
        keyval_base * gain_one,
        out_weight_grad,
        ffn_gain_grad,
        gate_weight_grad,
        up_weight_grad,
        down_rows.T,
    )


def solution(mesh):
    axes = (X,) + R
    cut = Mesh(mesh.devices.reshape((PLANES,) + RANK_SIZES + (2,)), axes + (M,))
    return jax.shard_map(
        body,
        mesh=cut,
        in_specs=(
            P(axes, None),
            P(axes),
            P(axes, M),
            P(axes, None),
            P(M, axes),
            P(axes),
            P(axes, M),
            P(axes, M),
            P(M, axes),
            P(),
            P(axes, None),
        ),
        out_specs=(
            P(axes, None),
            P(axes, None),
            P(axes),
            P(axes, M),
            P(axes, None),
            P(M, axes),
            P(axes),
            P(axes, M),
            P(axes, M),
            P(M, axes),
        ),
        check_vma=False,
    )
```

```python
import functools

import jax
import jax.numpy as jnp
from jax import lax
from jax.experimental import pallas as pl
from jax.experimental.pallas import tpu as pltpu
from jax.sharding import Mesh, PartitionSpec as P

HD = 256
WINDOW = 2048
EPS = 1e-06

PLANES = 4
RANK_SIZES = (2, 4, 2)
RANKS = 16
CHIPS = 8
X = "x"
R = ("yl", "z", "c")
CHIP = ("yl", "z")
CORE = "c"
M = "mp"

F32 = jnp.float32
BF16 = jnp.bfloat16


def after(value, *earlier):
    return lax.optimization_barrier((value,) + earlier)[0]


def rms_scale(values):
    return lax.rsqrt(jnp.mean(values * values, axis=-1, keepdims=True) + EPS)


def norm_back(values, scale_rows, weighted):
    return scale_rows * weighted - values * scale_rows**3 * jnp.mean(
        weighted * values, axis=-1, keepdims=True
    )


def to_plane(block, shift):
    return lax.ppermute(block, X, [(i, (i + shift) % PLANES) for i in range(PLANES)])


def swap(block):
    return lax.ppermute(block, M, [(0, 1), (1, 0)])


def swap_cores(block):
    return lax.ppermute(block, CORE, [(0, 1), (1, 0)])


def rounded(values):
    return lax.reduce_precision(values, 8, 7).astype(BF16)


def sum_mp(part):
    low = rounded(part)
    return low.astype(F32) + swap(low).astype(F32)


def gather_planes(block):
    half = block.shape[0] // 2
    after = to_plane(block, -1)
    before = to_plane(block, 1)
    far_top = to_plane(before[:half], 1)
    far_low = to_plane(after[half:], -1)
    return jnp.concatenate([block, after, far_top, far_low, before], 0)


def collect_planes(block):
    return [block, to_plane(block, 3), to_plane(block, 2), to_plane(block, 1)]


def reduce_far(part):
    rows = part.shape[0] // PLANES
    half = rows // 2
    own, after_one, far, before_one = (
        part[i * rows : (i + 1) * rows].astype(F32) for i in range(PLANES)
    )
    far = rounded(far)
    top = to_plane(far[:half], 1).astype(F32)
    low = to_plane(far[half:], -1).astype(F32)
    after_one = jnp.concatenate([after_one[:half] + top, after_one[half:]], 0)
    before_one = jnp.concatenate([before_one[:half], before_one[half:] + low], 0)
    return own, rounded(after_one), rounded(before_one)


def reduce_near(own, after_one, before_one):
    return own + to_plane(before_one, -1).astype(F32) + to_plane(after_one, 1).astype(F32)


def reduce_planes(part):
    return reduce_near(*reduce_far(part))


def pick(blocks, index):
    return lax.dynamic_index_in_dim(blocks, lax.rem(index + PLANES, PLANES), 0, keepdims=False)


def natural(blocks):
    plane = lax.axis_index(X)
    return [pick(blocks, p - plane) for p in range(PLANES)]


def send_planes(blocks):
    plane = lax.axis_index(X)
    return [pick(blocks, plane)] + [
        to_plane(pick(blocks, plane + k), k) for k in range(1, PLANES)
    ]


def exchange_planes(blocks):
    plane = lax.axis_index(X)
    got = jnp.stack(send_planes(blocks))
    return [pick(got, plane - p) for p in range(PLANES)]


def cut_planes(values):
    rows, width = values.shape
    got = send_planes(values.reshape(rows, PLANES, width // PLANES).swapaxes(0, 1))
    return jnp.concatenate([got[0], got[3], got[2], got[1]], 0)


def cut_features(blocks):
    got = send_planes(blocks)
    return [got[0], got[3], got[2], got[1]]


def join_planes(blocks):
    got = jnp.stack([blocks[0]] + [to_plane(blocks[k], k) for k in range(1, PLANES)])
    plane = lax.axis_index(X)
    return jnp.concatenate([pick(got, plane - p) for p in range(PLANES)], 1)


def permute_features(values):
    rows, width = values.shape
    cut = values.reshape(rows, PLANES, RANKS, width // (PLANES * RANKS))
    return cut.swapaxes(1, 2).reshape(rows, width)


def restore_features(values):
    rows, width = values.shape
    cut = values.reshape(rows, RANKS, PLANES, width // (PLANES * RANKS))
    return cut.swapaxes(1, 2).reshape(rows, width)


def spread(block, axes, size):
    rows, columns = block.shape
    copies = jnp.broadcast_to(block[None], (size, rows, columns)).reshape(size * rows, columns)
    return lax.all_to_all(copies, axes, 0, 0, tiled=True)


def gather_rows(block):
    return lax.all_gather(block, R, axis=0, tiled=True)


def dot_rows(left, right):
    return lax.dot_general(left, right, (((1,), (1,)), ((), ())), preferred_element_type=F32)


def dot_tokens(left, right):
    return lax.dot_general(left, right, (((0,), (0,)), ((), ())), preferred_element_type=F32)


def softmax_parts(query, parts, biases):
    scale = HD ** (-0.5)
    scores = [dot_rows(query, part[0]) * scale + bias[...] for part, bias in zip(parts, biases)]
    top = functools.reduce(
        jnp.maximum, [jnp.max(score, axis=-1, keepdims=True) for score in scores]
    )
    scores = [jnp.exp(score - top) for score in scores]
    inverse = 1.0 / sum(jnp.sum(score, axis=-1, keepdims=True) for score in scores)
    return [score * inverse for score in scores]


def attend_kernel(count, query, *refs):
    parts, biases, out = refs[:count], refs[count : 2 * count], refs[2 * count]
    weights = softmax_parts(query[...], parts, biases)
    out[...] = sum(
        jnp.dot(weight.astype(BF16), part[1], preferred_element_type=F32)
        for weight, part in zip(weights, parts)
    ).astype(out.dtype)


def attend_back_kernel(
    core, query, out_grad, attended, token_scale, *refs
):
    parts, biases, refs = refs[:3], refs[3:6], refs[6:]
    both, window_grad, last_grad, refs = refs[0], refs[1], refs[2], refs[3:]
    queries, out_grads, refs = refs[0], refs[1], refs[2:]
    weights_all, scores_all = refs[:3], refs[3:]
    head = pl.program_id(0)
    heads = pl.num_programs(0)
    rows = query.shape[0]
    here = pl.ds(pl.multiple_of(head * rows, rows), rows)
    scale = HD ** (-0.5)
    weights = softmax_parts(query[...], parts, biases)
    grad = out_grad[...]
    probs = [dot_rows(grad, part[1]) for part in parts]
    inner = sum(
        jnp.sum(weight * prob, axis=-1, keepdims=True) for weight, prob in zip(weights, probs)
    )
    scores = [
        (weight * (prob - inner)).astype(BF16) for weight, prob in zip(weights, probs)
    ]
    both[:, pl.ds(pl.multiple_of(head * HD, HD), HD)] = (
        sum(
            jnp.dot(score, part[0], preferred_element_type=F32)
            for score, part in zip(scores, parts)
        )
        * (token_scale[...] * scale)
    ).astype(both.dtype)
    both[:, pl.ds(pl.multiple_of((heads + head) * HD, HD), HD)] = attended[...]
    queries[here, :] = query[...]
    out_grads[here, :] = grad
    for i in range(3):
        weights_all[i][here, :] = weights[i].astype(BF16)
        scores_all[i][here, :] = scores[i]

    @pl.when(head == heads - 1)
    def _():
        for i in range(3):
            key = (dot_tokens(scores_all[i][...], queries[...]) * scale).astype(BF16)
            value = dot_tokens(weights_all[i][...], out_grads[...]).astype(BF16)
            if i == 2:
                last_grad[0] = key
                last_grad[1] = value
            else:
                which = core[0] if i == 0 else 1 - core[0]
                shape = (CHIPS, 1, rows, HD)
                window_grad[0, :, pl.ds(which, 1)] = key.reshape(shape)
                window_grad[1, :, pl.ds(which, 1)] = value.reshape(shape)


def whole_spec(shape):
    return pl.BlockSpec(shape, lambda i: (0,) * len(shape))


def attend(queries, parts, biases):
    rows, width = queries.shape
    span = sum(bias.shape[1] for bias in biases)
    head_spec = pl.BlockSpec((rows, HD), lambda i: (0, i))
    return pl.pallas_call(
        functools.partial(attend_kernel, len(parts)),
        grid=(width // HD,),
        in_specs=[head_spec] + [whole_spec(v.shape) for v in (*parts, *biases)],
        out_specs=head_spec,
        out_shape=jax.ShapeDtypeStruct(queries.shape, BF16),
        compiler_params=pltpu.CompilerParams(vmem_limit_bytes=48 * 1024 * 1024),
        cost_estimate=pl.CostEstimate(
            flops=4 * rows * width * span,
            bytes_accessed=4 * span * HD + 4 * rows * span + 4 * queries.size,
            transcendentals=rows * span * (width // HD),
        ),
    )(queries, *parts, *biases)


def attend_back(core, queries, out_grad, attended, token_scale, parts, biases):
    rows, width = queries.shape
    heads = width // HD
    spans = [bias.shape[1] for bias in biases]
    head_spec = pl.BlockSpec((rows, HD), lambda i: (0, i))
    shapes = [(rows, 2 * width), (2, CHIPS, 2, rows, HD), parts[-1].shape]
    return pl.pallas_call(
        attend_back_kernel,
        grid=(heads,),
        in_specs=[pl.BlockSpec(memory_space=pltpu.SMEM), head_spec, head_spec, head_spec]
        + [whole_spec(v.shape) for v in (token_scale, *parts, *biases)],
        out_specs=[whole_spec(shape) for shape in shapes],
        out_shape=[jax.ShapeDtypeStruct(shape, BF16) for shape in shapes],
        scratch_shapes=[pltpu.VMEM((heads * rows, HD), BF16)] * 2
        + [pltpu.VMEM((heads * rows, span), BF16) for span in spans] * 2,
        compiler_params=pltpu.CompilerParams(vmem_limit_bytes=56 * 1024 * 1024),
        cost_estimate=pl.CostEstimate(
            flops=10 * rows * width * sum(spans),
            bytes_accessed=8 * sum(spans) * HD + 4 * rows * sum(spans) + 6 * queries.size,
            transcendentals=rows * sum(spans) * heads,
        ),
    )(core.reshape(1), queries, out_grad, attended, token_scale, *parts, *biases)


def geglu_kernel(tokens, cot, gate_weight, up_weight, down_weight, hidden, gate_up):
    step = pl.program_id(0)
    block = gate_weight.shape[1]
    gate = jnp.dot(tokens[...], gate_weight[...], preferred_element_type=F32)
    up = jnp.dot(tokens[...], up_weight[...], preferred_element_type=F32)
    hidden_grad = jnp.dot(cot[...], down_weight[...], preferred_element_type=F32)
    hidden_grad = hidden_grad.astype(BF16).astype(F32)
    root = 0.7978845608028654
    square = gate * gate
    bend = jnp.tanh(root * gate * (1.0 + 0.044715 * square))
    half = 0.5 * (1.0 + bend)
    gelu = gate * half
    slope = half + 0.5 * gate * (1.0 - bend * bend) * (root * (1.0 + 3 * 0.044715 * square))
    here = pl.ds(pl.multiple_of(step * block, block), block)
    hidden[:, here] = (gelu * up).astype(BF16)
    gate_up[:, here] = (hidden_grad * up * slope).astype(BF16)
    there = pl.ds(pl.multiple_of(hidden.shape[1] + step * block, block), block)
    gate_up[:, there] = (hidden_grad * gelu).astype(BF16)


def geglu(tokens, cot, weights):
    rows, width = tokens.shape
    units = weights.shape[1] // 3
    block = 256 if units % 256 == 0 else 128
    steps = units // block
    token_spec = pl.BlockSpec(tokens.shape, lambda i: (0, 0), pipeline_mode=pl.Buffered(1))
    return pl.pallas_call(
        geglu_kernel,
        grid=(steps,),
        in_specs=[
            token_spec,
            token_spec,
            pl.BlockSpec((width, block), lambda i: (0, i)),
            pl.BlockSpec((width, block), lambda i: (0, steps + i)),
            pl.BlockSpec((width, block), lambda i: (0, 2 * steps + i)),
        ],
        out_specs=[whole_spec((rows, units)), whole_spec((rows, 2 * units))],
        out_shape=[
            jax.ShapeDtypeStruct((rows, units), BF16),
            jax.ShapeDtypeStruct((rows, 2 * units), BF16),
        ],
        compiler_params=pltpu.CompilerParams(vmem_limit_bytes=56 * 1024 * 1024),
        cost_estimate=pl.CostEstimate(
            flops=2 * rows * width * 3 * units,
            bytes_accessed=2 * weights.size + 4 * tokens.size + 6 * rows * units,
            transcendentals=rows * units,
        ),
    )(tokens, cot, weights, weights, weights)


def outer_kernel(count, *refs):
    out = refs[-1]
    first = 0
    for i in range(count):
        left, right = refs[2 * i], refs[2 * i + 1]
        columns = right.shape[1]
        tokens_first = left.shape[0] == right.shape[0]
        step = 512 if columns % 512 == 0 else columns
        for at in range(0, columns, step):
            out[:, first + at : first + at + step] = lax.dot_general(
                left[...],
                right[:, at : at + step],
                (((0 if tokens_first else 1,), (0,)), ((), ())),
                preferred_element_type=F32,
            ).astype(out.dtype)
        first += columns


def token_outer(*pairs):
    tokens, height = pairs[0][0].shape
    columns = sum(right.shape[1] for _, right in pairs)
    block = next(size for size in (512, 640, 256, 128) if height % size == 0)
    specs, operands = [], []
    for left, right in pairs:
        specs += [
            pl.BlockSpec((tokens, block), lambda i: (0, i))
            if left.shape[0] == tokens
            else pl.BlockSpec((block, tokens), lambda i: (i, 0)),
            pl.BlockSpec(right.shape, lambda i: (0, 0)),
        ]
        operands += [left, right]
    return pl.pallas_call(
        functools.partial(outer_kernel, len(pairs)),
        grid=(height // block,),
        in_specs=specs,
        out_specs=pl.BlockSpec((block, columns), lambda i: (i, 0)),
        out_shape=jax.ShapeDtypeStruct((height, columns), BF16),
        compiler_params=pltpu.CompilerParams(vmem_limit_bytes=40 * 1024 * 1024),
        cost_estimate=pl.CostEstimate(
            flops=2 * tokens * height * columns,
            bytes_accessed=2 * height * columns + 2 * tokens * (height * len(pairs) + columns),
            transcendentals=0,
        ),
    )(*operands)


def attn_outer_kernel(*refs):
    inputs, cuts, boths = refs[0], refs[1:5], refs[5:9]
    out = refs[9]
    rows, width = boths[0].shape[0], boths[0].shape[1] // 2
    out[:, :width] = sum(
        dot_tokens(inputs[k * rows : (k + 1) * rows, :], boths[k][:, :width])
        for k in range(PLANES)
    ).astype(out.dtype)
    out[:, width:] = sum(
        jnp.dot(cuts[k][...], boths[k][:, width:], preferred_element_type=F32)
        for k in range(PLANES)
    ).astype(out.dtype)


def attn_outer(inputs, cuts, boths):
    height, columns = inputs.shape[1], boths[0].shape[1]
    rows = boths[0].shape[0]
    block = 128
    return pl.pallas_call(
        attn_outer_kernel,
        grid=(height // block,),
        in_specs=[pl.BlockSpec((inputs.shape[0], block), lambda i: (0, i))]
        + [pl.BlockSpec((block, rows), lambda i: (i, 0))] * PLANES
        + [whole_spec(boths[0].shape)] * PLANES,
        out_specs=pl.BlockSpec((block, columns), lambda i: (i, 0)),
        out_shape=jax.ShapeDtypeStruct((height, columns), BF16),
        compiler_params=pltpu.CompilerParams(vmem_limit_bytes=40 * 1024 * 1024),
        cost_estimate=pl.CostEstimate(
            flops=2 * PLANES * rows * height * columns,
            bytes_accessed=2 * (height + PLANES * rows) * columns + 4 * inputs.size,
            transcendentals=0,
        ),
    )(inputs, *cuts, *boths)


def input_back_kernel(*refs):
    boths, keyvals, query_rows, keyval_rows = refs[:4], refs[4:8], refs[8], refs[9]
    keyval_out, outs = refs[10], refs[11:]
    rows, width = boths[0].shape[0], boths[0].shape[1] // 2
    for k in range(PLANES):
        keyval = (
            keyvals[k][:rows].astype(F32) + keyvals[(k + 1) % PLANES][rows:].astype(F32)
        ).astype(BF16)
        keyval_out[k * rows : (k + 1) * rows] = keyval
        outs[k][...] = (
            dot_rows(boths[k][:, :width], query_rows[...]) + dot_rows(keyval, keyval_rows[...])
        ).astype(outs[k].dtype)


def input_back(boths, keyvals, query_rows, keyval_rows):
    rows = boths[0].shape[0]
    height = query_rows.shape[0]
    shapes = [(PLANES * rows, HD)] + [(rows, height)] * PLANES
    operands = (*boths, *keyvals, query_rows, keyval_rows)
    return pl.pallas_call(
        input_back_kernel,
        grid=(1,),
        in_specs=[whole_spec(v.shape) for v in operands],
        out_specs=[whole_spec(shape) for shape in shapes],
        out_shape=[jax.ShapeDtypeStruct(shape, BF16) for shape in shapes],
        compiler_params=pltpu.CompilerParams(vmem_limit_bytes=40 * 1024 * 1024),
        cost_estimate=pl.CostEstimate(
            flops=2 * PLANES * rows * height * query_rows.shape[1],
            bytes_accessed=2 * sum(v.size for v in operands) + 2 * PLANES * rows * height,
            transcendentals=0,
        ),
    )(*operands)


def join_kernel(padded, gate_weight, up_weight, gain, *refs):
    pieces, outs, gain_out = refs[:PLANES], refs[PLANES : PLANES + 3], refs[PLANES + 3]
    units = gate_weight.shape[1] // PLANES
    total = jnp.zeros((gate_weight.shape[0], 1), F32)
    for p in range(PLANES):
        columns = slice(p * units, (p + 1) * units)
        gate = pieces[p][:, :units].astype(F32)
        up = pieces[p][:, padded : padded + units].astype(F32)
        total += jnp.sum(
            gate_weight[:, columns].astype(F32) * gate + up_weight[:, columns].astype(F32) * up,
            axis=1,
            keepdims=True,
        )
        outs[0][:, columns] = gate * gain[...]
        outs[1][:, columns] = up * gain[...]
        outs[2][:, columns] = pieces[p][:, 2 * padded : 2 * padded + units].astype(F32)
    gain_out[...] = total


def join(pieces, gate_weight, up_weight, gain):
    shape = gate_weight.shape
    padded = pieces[0].shape[1] // 3
    operands = (gate_weight, up_weight, gain, *pieces)
    shapes = [shape] * 3 + [(shape[0], 1)]
    return pl.pallas_call(
        functools.partial(join_kernel, padded),
        grid=(1,),
        in_specs=[whole_spec(v.shape) for v in operands],
        out_specs=[whole_spec(one) for one in shapes],
        out_shape=[jax.ShapeDtypeStruct(one, F32) for one in shapes],
        compiler_params=pltpu.CompilerParams(vmem_limit_bytes=40 * 1024 * 1024),
        cost_estimate=pl.CostEstimate(
            flops=10 * gate_weight.size,
            bytes_accessed=24 * gate_weight.size,
            transcendentals=0,
        ),
    )(*operands)


def body(
    inputs,
    attn_gain,
    query_weight,
    keyval_weight,
    out_weight,
    ffn_gain,
    gate_weight,
    up_weight,
    down_weight,
    positions,
    cotangent,
):
    rows, width = inputs.shape
    own = attn_gain.shape[0]
    query_width = query_weight.shape[1]
    head_count = query_width // HD
    units = gate_weight.shape[1] // PLANES
    padded = -(-units // 128) * 128
    scale = HD ** (-0.5)
    plane = lax.axis_index(X)
    rank = lax.axis_index(R)
    half = lax.axis_index(M)
    core = lax.axis_index(CORE)
    chip = lax.axis_index(CHIP)
    chips = jnp.arange(CHIPS, dtype=jnp.int32)
    ahead = (chips >= chip)[:, None, None]
    at_home = (chips == chip)[:, None, None]
    gain_one = attn_gain.astype(F32)[:, None]
    gain_two = ffn_gain.astype(F32)[:, None]

    keyval_own = (
        lax.dynamic_slice_in_dim(keyval_weight, half * HD, HD, 1).astype(F32) * gain_one
    ).astype(BF16)
    query_own = (query_weight.astype(F32) * gain_one).astype(BF16)
    inputs_cut = cut_planes(inputs)
    tokens_in = inputs.astype(F32)
    scale_attn = rms_scale(tokens_in)
    scale_before = to_plane(scale_attn.reshape(1, rows), 1).reshape(rows, 1)

    def cut(weight):
        blocks = weight.reshape(own, PLANES, units)
        return jnp.pad(blocks, ((0, 0), (0, 0), (0, padded - units))).swapaxes(0, 1)

    ffn_own = jnp.concatenate(
        [
            cut((gate_weight.astype(F32) * gain_two).astype(BF16)),
            cut((up_weight.astype(F32) * gain_two).astype(BF16)),
            cut(down_weight.T),
        ],
        2,
    ).reshape(PLANES * own, 3 * padded)
    out_planes = lax.all_gather(out_weight.T, X, axis=0, tiled=True)
    both = gather_rows(jnp.concatenate([query_own, out_planes], 0))
    ffn_own = lax.all_to_all(after(ffn_own, out_planes), X, 0, 0, tiled=True)
    ffn = gather_rows(ffn_own)
    keyval_rows = spread(after(keyval_own, ffn_own), R, RANKS)

    ranks = jnp.arange(RANKS, dtype=jnp.int32)
    block_own = plane * RANKS + rank
    offsets = jnp.arange(rows, dtype=jnp.int32)
    span = RANKS * rows
    pos_own = lax.dynamic_slice_in_dim(positions, plane * span, span, 0).reshape(RANKS, rows)
    pos_before = lax.dynamic_slice_in_dim(
        positions, jnp.maximum(plane - 1, 0) * span, span, 0
    ).reshape(RANKS, rows)
    pos_last = lax.dynamic_slice_in_dim(pos_before, rank, 1, 0)
    def in_parts(own_values, before_values, last_values):
        chosen = jnp.where((ranks <= rank)[:, None], own_values, before_values)
        cores = chosen.reshape(CHIPS, 2, rows)
        parts = [
            lax.dynamic_index_in_dim(cores, index, 1, keepdims=False).reshape(-1)
            for index in (core, 1 - core)
        ]
        return jnp.concatenate(parts + [last_values.reshape(-1)])

    index_own = ((plane * RANKS + ranks) * rows)[:, None] + offsets[None]
    key_index = in_parts(
        index_own, index_own - span, (block_own - RANKS) * rows + offsets
    )
    pos_keys = in_parts(pos_own, pos_before, pos_last)
    pos_query = lax.dynamic_slice_in_dim(positions, block_own * rows, rows, 0)
    query_index = block_own * rows + offsets
    allowed = (
        (key_index[None, :] >= 0)
        & (key_index[None, :] <= query_index[:, None])
        & (pos_query[:, None] - pos_keys[None, :] < WINDOW)
    )

    bias = jnp.where(allowed, 0.0, -1e30)
    part_span = CHIPS * rows
    biases = [
        bias[:, :part_span],
        bias[:, part_span : 2 * part_span],
        bias[:, 2 * part_span :],
    ]
    residual, cot = lax.optimization_barrier(
        (
            permute_features(after(inputs, ffn_own)),
            permute_features(after(cotangent, ffn_own)),
        )
    )

    keyval = (
        reduce_planes(
            jnp.dot(
                after(inputs_cut, residual, cot),
                keyval_rows,
                preferred_element_type=F32,
            )
        )
        * scale_attn
    ).astype(BF16)
    keyval_before = to_plane(keyval, 1)
    before_other = to_plane(swap(keyval), 1)
    down = ffn[:, 2 * padded :]

    both = both.reshape(RANKS, (1 + PLANES) * own, query_width)
    query_rows = lax.optimization_barrier(both[:, :own].reshape(RANKS * own, query_width))
    out_rows = both[:, own:].reshape(width, query_width)
    queries_part = jnp.dot(after(inputs_cut, before_other), query_rows, preferred_element_type=F32)
    queries_sum = reduce_planes(queries_part)
    first = half == 0
    last = jnp.where(
        first,
        jnp.stack([keyval_before, before_other]),
        jnp.stack([before_other, keyval_before]),
    )
    chosen = jnp.where(ahead, keyval[None], keyval_before[None])
    sent = jnp.broadcast_to(chosen[None], (2, CHIPS, rows, HD))
    met = lax.all_to_all(
        sent.reshape(2 * CHIPS * rows, HD), (M,) + CHIP, 0, 0, tiled=True
    ).reshape(2, CHIPS, rows, HD)
    met_lent = jnp.where(at_home & (core == 1), last[:, None], met)
    met_other = swap_cores(after(met_lent, queries_sum))
    window = [v.reshape(2, CHIPS * rows, HD) for v in (met, met_other)]
    queries, out_rows = lax.optimization_barrier(
        ((queries_sum * scale_attn).astype(BF16), out_rows)
    )

    attended = attend(queries, window + [last], biases)
    branch_part = jnp.einsum("te,de->td", attended, out_rows, preferred_element_type=F32)
    branch = sum_mp(branch_part)
    cot_all = gather_planes(after(cot, queries))
    middle = residual.astype(F32) + after(branch, cot_all)

    scale_ffn = rms_scale(middle)
    normed = (middle * scale_ffn).astype(BF16)
    normed_all = gather_planes(normed)
    hidden, gate_up_low = geglu(normed_all, cot_all, ffn)
    ffn_grad_part = token_outer((normed_all, gate_up_low), (cot_all, hidden))
    ffn_grad_rows = lax.psum_scatter(ffn_grad_part, R, scatter_dimension=0, tiled=True)
    gate_up_low = after(gate_up_low, ffn_grad_part)
    weighted_part = jnp.einsum(
        "tf,ef->te", gate_up_low, ffn[:, : 2 * padded], preferred_element_type=F32
    ).astype(BF16)
    weighted_low = rounded(reduce_planes(weighted_part))
    weighted = weighted_low.astype(F32) + swap(weighted_low).astype(F32)

    middle_grad = cot.astype(F32) + norm_back(middle, scale_ffn, weighted)
    branch_low = middle_grad.astype(BF16)
    attended_grad = jnp.dot(branch_low, out_rows, preferred_element_type=F32).astype(BF16)
    query_both, window_grad, last_grad = attend_back(
        core, queries, attended_grad, attended, scale_attn, window + [last], biases
    )
    gathered = collect_planes(query_both)
    branch_late = after(branch_low, *gathered)
    branch_turned = branch_late.T.reshape(RANKS, PLANES, own, rows)
    branch_cut = cut_features(branch_turned.swapaxes(0, 1).reshape(PLANES, RANKS * own, rows))

    ffn_part = jnp.einsum(
        "tf,ef->te", after(hidden, *branch_cut), down, preferred_element_type=F32
    )
    ffn_low = rounded(reduce_planes(ffn_part))

    returned = lax.all_to_all(
        window_grad.reshape(2 * RANKS * rows, HD), (M,) + R, 0, 0, tiled=True
    ).reshape(2, RANKS, rows, HD)
    last_other = swap(jnp.where(first, last_grad[1], last_grad[0]))
    last_mine = jnp.where(first, last_grad[0], last_grad[1])
    own_plane = (ranks >= rank)[:, None, None]
    own_sum = jnp.sum(jnp.where(own_plane, returned, 0).astype(F32), (0, 1))
    before_sum = (
        jnp.sum(jnp.where(own_plane, 0, returned).astype(F32), (0, 1))
        + last_mine.astype(F32)
        + last_other.astype(F32)
    )

    keyval_pieces = collect_planes(
        rounded(jnp.concatenate([own_sum * scale_attn, before_sum * scale_before], 0))
    )
    attn_grad_part = attn_outer(inputs_cut, branch_cut, gathered)
    attn_width = attn_grad_part.shape[1]
    attn_cores = attn_grad_part.reshape(CHIPS, 2, own, attn_width)
    attn_lent = swap_cores(lax.dynamic_index_in_dim(attn_cores, 1 - core, 1, keepdims=False))
    attn_kept = lax.dynamic_index_in_dim(attn_cores, core, 1, keepdims=False)
    attn_chip = rounded(attn_kept.astype(F32) + attn_lent.astype(F32))
    attn_met = lax.all_to_all(
        attn_chip.reshape(CHIPS * own, attn_width), CHIP, 0, 0, tiled=True
    )
    keyval_all, *input_parts = input_back(gathered, keyval_pieces, query_rows, keyval_rows)
    ffn_grad_rows, middle_late, ffn_low, attn_met = lax.optimization_barrier(
        (ffn_grad_rows, middle_grad, ffn_low, attn_met)
    )
    input_parts[1] = after(input_parts[1], attn_met)
    weighted_low = rounded(join_planes(input_parts).astype(F32))
    weighted_other = swap(weighted_low)
    ffn_grad_rows = after(ffn_grad_rows, weighted_low)
    attn_base = jnp.sum(attn_met.reshape(CHIPS, own, attn_width).astype(F32), 0)
    query_base = attn_base[:, :query_width]
    out_weight_grad = attn_base[:, query_width : 2 * query_width].T
    keyval_met = lax.all_to_all(
        after(token_outer((inputs_cut, keyval_all)), attn_met), R, 0, 0, tiled=True
    )
    keyval_mine = jnp.sum(keyval_met.reshape(RANKS, own, HD).astype(F32), 0)
    keyval_other = swap(after(keyval_mine, weighted_other))
    keyval_base = jnp.concatenate(
        [
            jnp.where(first, keyval_mine, keyval_other),
            jnp.where(first, keyval_other, keyval_mine),
        ],
        1,
    )

    weighted_one = weighted_low.astype(F32) + weighted_other.astype(F32)
    input_grad = (
        restore_features(middle_late)
        + weighted_one
        - tokens_in
        * scale_attn**2
        * jnp.mean(weighted_one * tokens_in, axis=-1, keepdims=True)
    )

    ffn_sum = ffn_low.astype(F32) + swap(ffn_low).astype(F32)
    activations = restore_features((middle + ffn_sum).astype(BF16))
    ffn_grad_own = exchange_planes(ffn_grad_rows.reshape(PLANES, own, 3 * padded))
    gate_weight_grad, up_weight_grad, down_rows, ffn_gain_part = join(
        ffn_grad_own, gate_weight, up_weight, gain_two
    )

    gain_parts = jnp.stack(
        [jnp.sum(query_weight.astype(F32) * query_base, axis=1), ffn_gain_part[:, 0]]
    )
    gain_sums = gain_parts + swap(after(gain_parts, weighted_other))
    ffn_gain_grad = gain_sums[1]
    attn_gain_grad = gain_sums[0] + jnp.sum(keyval_weight.astype(F32) * keyval_base, axis=1)

    return (
        activations,
        input_grad,
        attn_gain_grad,
        query_base * gain_one,
        keyval_base * gain_one,
        out_weight_grad,
        ffn_gain_grad,
        gate_weight_grad,
        up_weight_grad,
        down_rows.T,
    )


def solution(mesh):
    axes = (X,) + R
    cut = Mesh(mesh.devices.reshape((PLANES,) + RANK_SIZES + (2,)), axes + (M,))
    return jax.shard_map(
        body,
        mesh=cut,
        in_specs=(
            P(axes, None),
            P(axes),
            P(axes, M),
            P(axes, None),
            P(M, axes),
            P(axes),
            P(axes, M),
            P(axes, M),
            P(M, axes),
            P(),
            P(axes, None),
        ),
        out_specs=(
            P(axes, None),
            P(axes, None),
            P(axes),
            P(axes, M),
            P(axes, None),
            P(M, axes),
            P(axes),
            P(axes, M),
            P(axes, M),
            P(M, axes),
        ),
        check_vma=False,
    )
```

```python
import functools

import jax
import jax.numpy as jnp
from jax import lax
from jax.experimental import pallas as pl
from jax.experimental.pallas import tpu as pltpu
from jax.sharding import Mesh, PartitionSpec as P

HD = 256
WINDOW = 2048
EPS = 1e-06

PLANES = 4
RANK_SIZES = (2, 4, 2)
RANKS = 16
CHIPS = 8
X = "x"
R = ("yl", "z", "c")
CHIP = ("yl", "z")
CORE = "c"
M = "mp"

F32 = jnp.float32
BF16 = jnp.bfloat16


def after(value, *earlier):
    return lax.optimization_barrier((value,) + earlier)[0]


def rms_scale(values):
    return lax.rsqrt(jnp.mean(values * values, axis=-1, keepdims=True) + EPS)


def norm_back(values, scale_rows, weighted):
    return scale_rows * weighted - values * scale_rows**3 * jnp.mean(
        weighted * values, axis=-1, keepdims=True
    )


def to_plane(block, shift):
    return lax.ppermute(block, X, [(i, (i + shift) % PLANES) for i in range(PLANES)])


def swap(block):
    return lax.ppermute(block, M, [(0, 1), (1, 0)])


def swap_cores(block):
    return lax.ppermute(block, CORE, [(0, 1), (1, 0)])


def rounded(values):
    return lax.reduce_precision(values, 8, 7).astype(BF16)


def sum_mp(part):
    low = rounded(part)
    return low.astype(F32) + swap(low).astype(F32)


def gather_planes(block):
    half = block.shape[0] // 2
    after = to_plane(block, -1)
    before = to_plane(block, 1)
    far_top = to_plane(before[:half], 1)
    far_low = to_plane(after[half:], -1)
    return jnp.concatenate([block, after, far_top, far_low, before], 0)


def collect_planes(block):
    return [block, to_plane(block, 3), to_plane(block, 2), to_plane(block, 1)]


def reduce_far(part):
    rows = part.shape[0] // PLANES
    half = rows // 2
    own, after_one, far, before_one = (
        part[i * rows : (i + 1) * rows].astype(F32) for i in range(PLANES)
    )
    far = rounded(far)
    top = to_plane(far[:half], 1).astype(F32)
    low = to_plane(far[half:], -1).astype(F32)
    after_one = jnp.concatenate([after_one[:half] + top, after_one[half:]], 0)
    before_one = jnp.concatenate([before_one[:half], before_one[half:] + low], 0)
    return own, rounded(after_one), rounded(before_one)


def reduce_near(own, after_one, before_one):
    return own + to_plane(before_one, -1).astype(F32) + to_plane(after_one, 1).astype(F32)


def reduce_planes(part):
    return reduce_near(*reduce_far(part))


def pick(blocks, index):
    return lax.dynamic_index_in_dim(blocks, lax.rem(index + PLANES, PLANES), 0, keepdims=False)


def natural(blocks):
    plane = lax.axis_index(X)
    return [pick(blocks, p - plane) for p in range(PLANES)]


def send_planes(blocks):
    plane = lax.axis_index(X)
    return [pick(blocks, plane)] + [
        to_plane(pick(blocks, plane + k), k) for k in range(1, PLANES)
    ]


def exchange_planes(blocks):
    plane = lax.axis_index(X)
    got = jnp.stack(send_planes(blocks))
    return [pick(got, plane - p) for p in range(PLANES)]


def cut_planes(values):
    rows, width = values.shape
    got = send_planes(values.reshape(rows, PLANES, width // PLANES).swapaxes(0, 1))
    return jnp.concatenate([got[0], got[3], got[2], got[1]], 0)


def cut_features(blocks):
    got = send_planes(blocks)
    return [got[0], got[3], got[2], got[1]]


def join_planes(blocks):
    got = jnp.stack([blocks[0]] + [to_plane(blocks[k], k) for k in range(1, PLANES)])
    plane = lax.axis_index(X)
    return jnp.concatenate([pick(got, plane - p) for p in range(PLANES)], 1)


def permute_features(values):
    rows, width = values.shape
    cut = values.reshape(rows, PLANES, RANKS, width // (PLANES * RANKS))
    return cut.swapaxes(1, 2).reshape(rows, width)


def restore_features(values):
    rows, width = values.shape
    cut = values.reshape(rows, RANKS, PLANES, width // (PLANES * RANKS))
    return cut.swapaxes(1, 2).reshape(rows, width)


def spread(block, axes, size):
    rows, columns = block.shape
    copies = jnp.broadcast_to(block[None], (size, rows, columns)).reshape(size * rows, columns)
    return lax.all_to_all(copies, axes, 0, 0, tiled=True)


def gather_rows(block):
    return lax.all_gather(block, R, axis=0, tiled=True)


def dot_rows(left, right):
    return lax.dot_general(left, right, (((1,), (1,)), ((), ())), preferred_element_type=F32)


def dot_tokens(left, right):
    return lax.dot_general(left, right, (((0,), (0,)), ((), ())), preferred_element_type=F32)


def softmax_parts(query, parts, biases):
    scale = HD ** (-0.5)
    scores = [dot_rows(query, part[0]) * scale + bias[...] for part, bias in zip(parts, biases)]
    top = functools.reduce(
        jnp.maximum, [jnp.max(score, axis=-1, keepdims=True) for score in scores]
    )
    scores = [jnp.exp(score - top) for score in scores]
    inverse = 1.0 / sum(jnp.sum(score, axis=-1, keepdims=True) for score in scores)
    return [score * inverse for score in scores]


def attend_kernel(count, query, *refs):
    parts, biases, out = refs[:count], refs[count : 2 * count], refs[2 * count]
    weights = softmax_parts(query[...], parts, biases)
    out[...] = sum(
        jnp.dot(weight.astype(BF16), part[1], preferred_element_type=F32)
        for weight, part in zip(weights, parts)
    ).astype(out.dtype)


def attend_back_kernel(
    core, query, out_grad, attended, token_scale, *refs
):
    parts, biases, refs = refs[:3], refs[3:6], refs[6:]
    both, window_grad, last_grad, refs = refs[0], refs[1], refs[2], refs[3:]
    queries, out_grads, refs = refs[0], refs[1], refs[2:]
    weights_all, scores_all = refs[:3], refs[3:]
    head = pl.program_id(0)
    heads = pl.num_programs(0)
    rows = query.shape[0]
    here = pl.ds(pl.multiple_of(head * rows, rows), rows)
    scale = HD ** (-0.5)
    weights = softmax_parts(query[...], parts, biases)
    grad = out_grad[...]
    probs = [dot_rows(grad, part[1]) for part in parts]
    inner = sum(
        jnp.sum(weight * prob, axis=-1, keepdims=True) for weight, prob in zip(weights, probs)
    )
    scores = [
        (weight * (prob - inner)).astype(BF16) for weight, prob in zip(weights, probs)
    ]
    both[:, pl.ds(pl.multiple_of(head * HD, HD), HD)] = (
        sum(
            jnp.dot(score, part[0], preferred_element_type=F32)
            for score, part in zip(scores, parts)
        )
        * (token_scale[...] * scale)
    ).astype(both.dtype)
    both[:, pl.ds(pl.multiple_of((heads + head) * HD, HD), HD)] = attended[...]
    queries[here, :] = query[...]
    out_grads[here, :] = grad
    for i in range(3):
        weights_all[i][here, :] = weights[i].astype(BF16)
        scores_all[i][here, :] = scores[i]

    @pl.when(head == heads - 1)
    def _():
        for i in range(3):
            key = (dot_tokens(scores_all[i][...], queries[...]) * scale).astype(BF16)
            value = dot_tokens(weights_all[i][...], out_grads[...]).astype(BF16)
            if i == 2:
                last_grad[0] = key
                last_grad[1] = value
            else:
                which = core[0] if i == 0 else 1 - core[0]
                shape = (CHIPS, 1, rows, HD)
                window_grad[0, :, pl.ds(which, 1)] = key.reshape(shape)
                window_grad[1, :, pl.ds(which, 1)] = value.reshape(shape)


def whole_spec(shape):
    return pl.BlockSpec(shape, lambda i: (0,) * len(shape))


def attend(queries, parts, biases):
    rows, width = queries.shape
    span = sum(bias.shape[1] for bias in biases)
    head_spec = pl.BlockSpec((rows, HD), lambda i: (0, i))
    return pl.pallas_call(
        functools.partial(attend_kernel, len(parts)),
        grid=(width // HD,),
        in_specs=[head_spec] + [whole_spec(v.shape) for v in (*parts, *biases)],
        out_specs=head_spec,
        out_shape=jax.ShapeDtypeStruct(queries.shape, BF16),
        compiler_params=pltpu.CompilerParams(vmem_limit_bytes=48 * 1024 * 1024),
        cost_estimate=pl.CostEstimate(
            flops=4 * rows * width * span,
            bytes_accessed=4 * span * HD + 4 * rows * span + 4 * queries.size,
            transcendentals=rows * span * (width // HD),
        ),
    )(queries, *parts, *biases)


def attend_back(core, queries, out_grad, attended, token_scale, parts, biases):
    rows, width = queries.shape
    heads = width // HD
    spans = [bias.shape[1] for bias in biases]
    head_spec = pl.BlockSpec((rows, HD), lambda i: (0, i))
    shapes = [(rows, 2 * width), (2, CHIPS, 2, rows, HD), parts[-1].shape]
    return pl.pallas_call(
        attend_back_kernel,
        grid=(heads,),
        in_specs=[pl.BlockSpec(memory_space=pltpu.SMEM), head_spec, head_spec, head_spec]
        + [whole_spec(v.shape) for v in (token_scale, *parts, *biases)],
        out_specs=[whole_spec(shape) for shape in shapes],
        out_shape=[jax.ShapeDtypeStruct(shape, BF16) for shape in shapes],
        scratch_shapes=[pltpu.VMEM((heads * rows, HD), BF16)] * 2
        + [pltpu.VMEM((heads * rows, span), BF16) for span in spans] * 2,
        compiler_params=pltpu.CompilerParams(vmem_limit_bytes=56 * 1024 * 1024),
        cost_estimate=pl.CostEstimate(
            flops=10 * rows * width * sum(spans),
            bytes_accessed=8 * sum(spans) * HD + 4 * rows * sum(spans) + 6 * queries.size,
            transcendentals=rows * sum(spans) * heads,
        ),
    )(core.reshape(1), queries, out_grad, attended, token_scale, *parts, *biases)


def geglu_kernel(
    steps, tokens, cot, gate_weight, up_weight, down_weight, hidden, gate_up, grads
):
    step = pl.program_id(0)
    block = gate_weight.shape[1]
    units = hidden.shape[1]

    @pl.when(step < steps)
    def _():
        gate = jnp.dot(tokens[...], gate_weight[...], preferred_element_type=F32)
        up = jnp.dot(tokens[...], up_weight[...], preferred_element_type=F32)
        hidden_grad = jnp.dot(cot[...], down_weight[...], preferred_element_type=F32)
        hidden_grad = hidden_grad.astype(BF16).astype(F32)
        root = 0.7978845608028654
        square = gate * gate
        bend = jnp.tanh(root * gate * (1.0 + 0.044715 * square))
        half = 0.5 * (1.0 + bend)
        gelu = gate * half
        slope = half + 0.5 * gate * (1.0 - bend * bend) * (root * (1.0 + 3 * 0.044715 * square))
        here = pl.ds(pl.multiple_of(step * block, block), block)
        hidden[:, here] = (gelu * up).astype(BF16)
        gate_up[:, here] = (hidden_grad * up * slope).astype(BF16)
        there = pl.ds(pl.multiple_of(units + step * block, block), block)
        gate_up[:, there] = (hidden_grad * gelu).astype(BF16)

    @pl.when(step >= steps)
    def _():
        height = grads.shape[0]
        rows = pl.ds(pl.multiple_of((step - steps) * height, 128), height)
        cut = 512 if units % 512 == 0 else 128
        for left, right, first in ((tokens, gate_up, 0), (cot, hidden, 2 * units)):
            for at in range(0, right.shape[1], cut):
                grads[:, first + at : first + at + cut] = dot_tokens(
                    left[:, rows], right[:, at : at + cut]
                ).astype(BF16)


def geglu(tokens, cot, weights):
    rows, width = tokens.shape
    units = weights.shape[1] // 3
    block = 256 if units % 256 == 0 else 128
    steps = units // block
    height = width // PLANES
    token_spec = pl.BlockSpec(tokens.shape, lambda i: (0, 0), pipeline_mode=pl.Buffered(1))

    def weight_spec(which):
        return pl.BlockSpec(
            (width, block), lambda i: (0, which * steps + jnp.minimum(i, steps - 1))
        )

    return pl.pallas_call(
        functools.partial(geglu_kernel, steps),
        grid=(steps + PLANES,),
        in_specs=[token_spec, token_spec] + [weight_spec(which) for which in range(3)],
        out_specs=[
            whole_spec((rows, units)),
            whole_spec((rows, 2 * units)),
            pl.BlockSpec((height, 3 * units), lambda i: (jnp.maximum(i - steps, 0), 0)),
        ],
        out_shape=[
            jax.ShapeDtypeStruct((rows, units), BF16),
            jax.ShapeDtypeStruct((rows, 2 * units), BF16),
            jax.ShapeDtypeStruct((width, 3 * units), BF16),
        ],
        compiler_params=pltpu.CompilerParams(vmem_limit_bytes=60 * 1024 * 1024),
        cost_estimate=pl.CostEstimate(
            flops=4 * rows * width * 3 * units,
            bytes_accessed=4 * weights.size + 4 * tokens.size + 6 * rows * units,
            transcendentals=rows * units,
        ),
    )(tokens, cot, weights, weights, weights)


def outer_kernel(count, *refs):
    out = refs[-1]
    first = 0
    for i in range(count):
        left, right = refs[2 * i], refs[2 * i + 1]
        columns = right.shape[1]
        tokens_first = left.shape[0] == right.shape[0]
        step = 512 if columns % 512 == 0 else columns
        for at in range(0, columns, step):
            out[:, first + at : first + at + step] = lax.dot_general(
                left[...],
                right[:, at : at + step],
                (((0 if tokens_first else 1,), (0,)), ((), ())),
                preferred_element_type=F32,
            ).astype(out.dtype)
        first += columns


def token_outer(*pairs):
    tokens, height = pairs[0][0].shape
    columns = sum(right.shape[1] for _, right in pairs)
    block = next(size for size in (512, 640, 256, 128) if height % size == 0)
    specs, operands = [], []
    for left, right in pairs:
        specs += [
            pl.BlockSpec((tokens, block), lambda i: (0, i))
            if left.shape[0] == tokens
            else pl.BlockSpec((block, tokens), lambda i: (i, 0)),
            pl.BlockSpec(right.shape, lambda i: (0, 0)),
        ]
        operands += [left, right]
    return pl.pallas_call(
        functools.partial(outer_kernel, len(pairs)),
        grid=(height // block,),
        in_specs=specs,
        out_specs=pl.BlockSpec((block, columns), lambda i: (i, 0)),
        out_shape=jax.ShapeDtypeStruct((height, columns), BF16),
        compiler_params=pltpu.CompilerParams(vmem_limit_bytes=40 * 1024 * 1024),
        cost_estimate=pl.CostEstimate(
            flops=2 * tokens * height * columns,
            bytes_accessed=2 * height * columns + 2 * tokens * (height * len(pairs) + columns),
            transcendentals=0,
        ),
    )(*operands)


def attn_outer_kernel(*refs):
    inputs, cuts, boths = refs[0], refs[1:5], refs[5:9]
    out = refs[9]
    rows, width = boths[0].shape[0], boths[0].shape[1] // 2
    out[:, :width] = sum(
        dot_tokens(inputs[k * rows : (k + 1) * rows, :], boths[k][:, :width])
        for k in range(PLANES)
    ).astype(out.dtype)
    out[:, width:] = sum(
        jnp.dot(cuts[k][...], boths[k][:, width:], preferred_element_type=F32)
        for k in range(PLANES)
    ).astype(out.dtype)


def attn_outer(inputs, cuts, boths):
    height, columns = inputs.shape[1], boths[0].shape[1]
    rows = boths[0].shape[0]
    block = 128
    return pl.pallas_call(
        attn_outer_kernel,
        grid=(height // block,),
        in_specs=[pl.BlockSpec((inputs.shape[0], block), lambda i: (0, i))]
        + [pl.BlockSpec((block, rows), lambda i: (i, 0))] * PLANES
        + [whole_spec(boths[0].shape)] * PLANES,
        out_specs=pl.BlockSpec((block, columns), lambda i: (i, 0)),
        out_shape=jax.ShapeDtypeStruct((height, columns), BF16),
        compiler_params=pltpu.CompilerParams(vmem_limit_bytes=40 * 1024 * 1024),
        cost_estimate=pl.CostEstimate(
            flops=2 * PLANES * rows * height * columns,
            bytes_accessed=2 * (height + PLANES * rows) * columns + 4 * inputs.size,
            transcendentals=0,
        ),
    )(inputs, *cuts, *boths)


def input_back_kernel(*refs):
    boths, keyvals, query_rows, keyval_rows = refs[:4], refs[4:8], refs[8], refs[9]
    keyval_out, outs = refs[10], refs[11:]
    rows, width = boths[0].shape[0], boths[0].shape[1] // 2
    for k in range(PLANES):
        keyval = (
            keyvals[k][:rows].astype(F32) + keyvals[(k + 1) % PLANES][rows:].astype(F32)
        ).astype(BF16)
        keyval_out[k * rows : (k + 1) * rows] = keyval
        outs[k][...] = (
            dot_rows(boths[k][:, :width], query_rows[...]) + dot_rows(keyval, keyval_rows[...])
        ).astype(outs[k].dtype)


def input_back(boths, keyvals, query_rows, keyval_rows):
    rows = boths[0].shape[0]
    height = query_rows.shape[0]
    shapes = [(PLANES * rows, HD)] + [(rows, height)] * PLANES
    operands = (*boths, *keyvals, query_rows, keyval_rows)
    return pl.pallas_call(
        input_back_kernel,
        grid=(1,),
        in_specs=[whole_spec(v.shape) for v in operands],
        out_specs=[whole_spec(shape) for shape in shapes],
        out_shape=[jax.ShapeDtypeStruct(shape, BF16) for shape in shapes],
        compiler_params=pltpu.CompilerParams(vmem_limit_bytes=40 * 1024 * 1024),
        cost_estimate=pl.CostEstimate(
            flops=2 * PLANES * rows * height * query_rows.shape[1],
            bytes_accessed=2 * sum(v.size for v in operands) + 2 * PLANES * rows * height,
            transcendentals=0,
        ),
    )(*operands)


def join_kernel(padded, gate_weight, up_weight, gain, *refs):
    pieces, outs, gain_out = refs[:PLANES], refs[PLANES : PLANES + 3], refs[PLANES + 3]
    units = gate_weight.shape[1] // PLANES
    total = jnp.zeros((gate_weight.shape[0], 1), F32)
    for p in range(PLANES):
        columns = slice(p * units, (p + 1) * units)
        gate = pieces[p][:, :units].astype(F32)
        up = pieces[p][:, padded : padded + units].astype(F32)
        total += jnp.sum(
            gate_weight[:, columns].astype(F32) * gate + up_weight[:, columns].astype(F32) * up,
            axis=1,
            keepdims=True,
        )
        outs[0][:, columns] = gate * gain[...]
        outs[1][:, columns] = up * gain[...]
        outs[2][:, columns] = pieces[p][:, 2 * padded : 2 * padded + units].astype(F32)
    gain_out[...] = total


def join(pieces, gate_weight, up_weight, gain):
    shape = gate_weight.shape
    padded = pieces[0].shape[1] // 3
    operands = (gate_weight, up_weight, gain, *pieces)
    shapes = [shape] * 3 + [(shape[0], 1)]
    return pl.pallas_call(
        functools.partial(join_kernel, padded),
        grid=(1,),
        in_specs=[whole_spec(v.shape) for v in operands],
        out_specs=[whole_spec(one) for one in shapes],
        out_shape=[jax.ShapeDtypeStruct(one, F32) for one in shapes],
        compiler_params=pltpu.CompilerParams(vmem_limit_bytes=40 * 1024 * 1024),
        cost_estimate=pl.CostEstimate(
            flops=10 * gate_weight.size,
            bytes_accessed=24 * gate_weight.size,
            transcendentals=0,
        ),
    )(*operands)


def body(
    inputs,
    attn_gain,
    query_weight,
    keyval_weight,
    out_weight,
    ffn_gain,
    gate_weight,
    up_weight,
    down_weight,
    positions,
    cotangent,
):
    rows, width = inputs.shape
    own = attn_gain.shape[0]
    query_width = query_weight.shape[1]
    head_count = query_width // HD
    units = gate_weight.shape[1] // PLANES
    padded = -(-units // 128) * 128
    scale = HD ** (-0.5)
    plane = lax.axis_index(X)
    rank = lax.axis_index(R)
    half = lax.axis_index(M)
    core = lax.axis_index(CORE)
    chip = lax.axis_index(CHIP)
    chips = jnp.arange(CHIPS, dtype=jnp.int32)
    ahead = (chips >= chip)[:, None, None]
    at_home = (chips == chip)[:, None, None]
    gain_one = attn_gain.astype(F32)[:, None]
    gain_two = ffn_gain.astype(F32)[:, None]

    keyval_own = (
        lax.dynamic_slice_in_dim(keyval_weight, half * HD, HD, 1).astype(F32) * gain_one
    ).astype(BF16)
    query_own = (query_weight.astype(F32) * gain_one).astype(BF16)
    inputs_cut = cut_planes(inputs)
    tokens_in = inputs.astype(F32)
    scale_attn = rms_scale(tokens_in)
    scale_before = to_plane(scale_attn.reshape(1, rows), 1).reshape(rows, 1)

    def cut(weight):
        blocks = weight.reshape(own, PLANES, units)
        return jnp.pad(blocks, ((0, 0), (0, 0), (0, padded - units))).swapaxes(0, 1)

    ffn_own = jnp.concatenate(
        [
            cut((gate_weight.astype(F32) * gain_two).astype(BF16)),
            cut((up_weight.astype(F32) * gain_two).astype(BF16)),
            cut(down_weight.T),
        ],
        2,
    ).reshape(PLANES * own, 3 * padded)
    out_planes = lax.all_gather(out_weight.T, X, axis=0, tiled=True)
    both = gather_rows(jnp.concatenate([query_own, out_planes], 0))
    ffn_own = lax.all_to_all(after(ffn_own, out_planes), X, 0, 0, tiled=True)
    ffn = gather_rows(ffn_own)
    keyval_rows = spread(after(keyval_own, ffn_own), R, RANKS)

    ranks = jnp.arange(RANKS, dtype=jnp.int32)
    block_own = plane * RANKS + rank
    offsets = jnp.arange(rows, dtype=jnp.int32)
    span = RANKS * rows
    pos_own = lax.dynamic_slice_in_dim(positions, plane * span, span, 0).reshape(RANKS, rows)
    pos_before = lax.dynamic_slice_in_dim(
        positions, jnp.maximum(plane - 1, 0) * span, span, 0
    ).reshape(RANKS, rows)
    pos_last = lax.dynamic_slice_in_dim(pos_before, rank, 1, 0)
    def in_parts(own_values, before_values, last_values):
        chosen = jnp.where((ranks <= rank)[:, None], own_values, before_values)
        cores = chosen.reshape(CHIPS, 2, rows)
        parts = [
            lax.dynamic_index_in_dim(cores, index, 1, keepdims=False).reshape(-1)
            for index in (core, 1 - core)
        ]
        return jnp.concatenate(parts + [last_values.reshape(-1)])

    index_own = ((plane * RANKS + ranks) * rows)[:, None] + offsets[None]
    key_index = in_parts(
        index_own, index_own - span, (block_own - RANKS) * rows + offsets
    )
    pos_keys = in_parts(pos_own, pos_before, pos_last)
    pos_query = lax.dynamic_slice_in_dim(positions, block_own * rows, rows, 0)
    query_index = block_own * rows + offsets
    allowed = (
        (key_index[None, :] >= 0)
        & (key_index[None, :] <= query_index[:, None])
        & (pos_query[:, None] - pos_keys[None, :] < WINDOW)
    )

    bias = jnp.where(allowed, 0.0, -1e30)
    part_span = CHIPS * rows
    biases = [
        bias[:, :part_span],
        bias[:, part_span : 2 * part_span],
        bias[:, 2 * part_span :],
    ]
    residual, cot = lax.optimization_barrier(
        (
            permute_features(after(inputs, ffn_own)),
            permute_features(after(cotangent, ffn_own)),
        )
    )

    keyval = (
        reduce_planes(
            jnp.dot(
                after(inputs_cut, residual, cot),
                keyval_rows,
                preferred_element_type=F32,
            )
        )
        * scale_attn
    ).astype(BF16)
    keyval_before = to_plane(keyval, 1)
    before_other = to_plane(swap(keyval), 1)
    down = ffn[:, 2 * padded :]

    both = both.reshape(RANKS, (1 + PLANES) * own, query_width)
    query_rows = lax.optimization_barrier(both[:, :own].reshape(RANKS * own, query_width))
    out_rows = both[:, own:].reshape(width, query_width)
    queries_part = jnp.dot(after(inputs_cut, before_other), query_rows, preferred_element_type=F32)
    queries_sum = reduce_planes(queries_part)
    first = half == 0
    last = jnp.where(
        first,
        jnp.stack([keyval_before, before_other]),
        jnp.stack([before_other, keyval_before]),
    )
    chosen = jnp.where(ahead, keyval[None], keyval_before[None])
    sent = jnp.broadcast_to(chosen[None], (2, CHIPS, rows, HD))
    met = lax.all_to_all(
        sent.reshape(2 * CHIPS * rows, HD), (M,) + CHIP, 0, 0, tiled=True
    ).reshape(2, CHIPS, rows, HD)
    met_lent = jnp.where(at_home & (core == 1), last[:, None], met)
    met_other = swap_cores(after(met_lent, queries_sum))
    window = [v.reshape(2, CHIPS * rows, HD) for v in (met, met_other)]
    queries, out_rows = lax.optimization_barrier(
        ((queries_sum * scale_attn).astype(BF16), out_rows)
    )

    attended = attend(queries, window + [last], biases)
    branch_part = jnp.einsum("te,de->td", attended, out_rows, preferred_element_type=F32)
    branch = sum_mp(branch_part)
    cot_all = gather_planes(after(cot, queries))
    middle = residual.astype(F32) + after(branch, cot_all)

    scale_ffn = rms_scale(middle)
    normed = (middle * scale_ffn).astype(BF16)
    normed_all = gather_planes(normed)
    hidden, gate_up_low, ffn_grad_part = geglu(normed_all, cot_all, ffn)
    ffn_grad_rows = lax.psum_scatter(ffn_grad_part, R, scatter_dimension=0, tiled=True)
    weighted_part = jnp.einsum(
        "tf,ef->te", gate_up_low, ffn[:, : 2 * padded], preferred_element_type=F32
    ).astype(BF16)
    weighted_low = rounded(reduce_planes(weighted_part))
    weighted = weighted_low.astype(F32) + swap(weighted_low).astype(F32)

    middle_grad = cot.astype(F32) + norm_back(middle, scale_ffn, weighted)
    branch_low = middle_grad.astype(BF16)
    attended_grad = jnp.dot(branch_low, out_rows, preferred_element_type=F32).astype(BF16)
    query_both, window_grad, last_grad = attend_back(
        core, queries, attended_grad, attended, scale_attn, window + [last], biases
    )
    gathered = collect_planes(query_both)
    branch_late = after(branch_low, *gathered)
    branch_turned = branch_late.T.reshape(RANKS, PLANES, own, rows)
    branch_cut = cut_features(branch_turned.swapaxes(0, 1).reshape(PLANES, RANKS * own, rows))

    ffn_part = jnp.einsum(
        "tf,ef->te", after(hidden, *branch_cut), down, preferred_element_type=F32
    )
    ffn_low = rounded(reduce_planes(ffn_part))

    returned = lax.all_to_all(
        window_grad.reshape(2 * RANKS * rows, HD), (M,) + R, 0, 0, tiled=True
    ).reshape(2, RANKS, rows, HD)
    last_other = swap(jnp.where(first, last_grad[1], last_grad[0]))
    last_mine = jnp.where(first, last_grad[0], last_grad[1])
    own_plane = (ranks >= rank)[:, None, None]
    own_sum = jnp.sum(jnp.where(own_plane, returned, 0).astype(F32), (0, 1))
    before_sum = (
        jnp.sum(jnp.where(own_plane, 0, returned).astype(F32), (0, 1))
        + last_mine.astype(F32)
        + last_other.astype(F32)
    )

    keyval_pieces = collect_planes(
        rounded(jnp.concatenate([own_sum * scale_attn, before_sum * scale_before], 0))
    )
    attn_grad_part = attn_outer(inputs_cut, branch_cut, gathered)
    attn_width = attn_grad_part.shape[1]
    attn_cores = attn_grad_part.reshape(CHIPS, 2, own, attn_width)
    attn_lent = swap_cores(lax.dynamic_index_in_dim(attn_cores, 1 - core, 1, keepdims=False))
    attn_kept = lax.dynamic_index_in_dim(attn_cores, core, 1, keepdims=False)
    attn_chip = rounded(attn_kept.astype(F32) + attn_lent.astype(F32))
    attn_met = lax.all_to_all(
        attn_chip.reshape(CHIPS * own, attn_width), CHIP, 0, 0, tiled=True
    )
    keyval_all, *input_parts = input_back(gathered, keyval_pieces, query_rows, keyval_rows)
    ffn_grad_rows, middle_late, ffn_low, attn_met = lax.optimization_barrier(
        (ffn_grad_rows, middle_grad, ffn_low, attn_met)
    )
    weighted_low = after(rounded(join_planes(input_parts).astype(F32)), attn_met)
    weighted_other = swap(weighted_low)
    ffn_grad_rows = after(ffn_grad_rows, weighted_low)
    attn_base = jnp.sum(attn_met.reshape(CHIPS, own, attn_width).astype(F32), 0)
    query_base = attn_base[:, :query_width]
    out_weight_grad = attn_base[:, query_width : 2 * query_width].T
    keyval_met = lax.all_to_all(
        after(token_outer((inputs_cut, keyval_all)), attn_met), R, 0, 0, tiled=True
    )
    keyval_mine = jnp.sum(keyval_met.reshape(RANKS, own, HD).astype(F32), 0)
    keyval_other = swap(after(keyval_mine, weighted_other))
    keyval_base = jnp.concatenate(
        [
            jnp.where(first, keyval_mine, keyval_other),
            jnp.where(first, keyval_other, keyval_mine),
        ],
        1,
    )

    weighted_one = weighted_low.astype(F32) + weighted_other.astype(F32)
    input_grad = (
        restore_features(middle_late)
        + weighted_one
        - tokens_in
        * scale_attn**2
        * jnp.mean(weighted_one * tokens_in, axis=-1, keepdims=True)
    )

    ffn_sum = ffn_low.astype(F32) + swap(ffn_low).astype(F32)
    activations = restore_features((middle + ffn_sum).astype(BF16))
    ffn_grad_own = exchange_planes(ffn_grad_rows.reshape(PLANES, own, 3 * padded))
    gate_weight_grad, up_weight_grad, down_rows, ffn_gain_part = join(
        ffn_grad_own, gate_weight, up_weight, gain_two
    )

    gain_parts = jnp.stack(
        [jnp.sum(query_weight.astype(F32) * query_base, axis=1), ffn_gain_part[:, 0]]
    )
    gain_sums = gain_parts + swap(after(gain_parts, weighted_other))
    ffn_gain_grad = gain_sums[1]
    attn_gain_grad = gain_sums[0] + jnp.sum(keyval_weight.astype(F32) * keyval_base, axis=1)

    return (
        activations,
        input_grad,
        attn_gain_grad,
        query_base * gain_one,
        keyval_base * gain_one,
        out_weight_grad,
        ffn_gain_grad,
        gate_weight_grad,
        up_weight_grad,
        down_rows.T,
    )


def solution(mesh):
    axes = (X,) + R
    cut = Mesh(mesh.devices.reshape((PLANES,) + RANK_SIZES + (2,)), axes + (M,))
    return jax.shard_map(
        body,
        mesh=cut,
        in_specs=(
            P(axes, None),
            P(axes),
            P(axes, M),
            P(axes, None),
            P(M, axes),
            P(axes),
            P(axes, M),
            P(axes, M),
            P(M, axes),
            P(),
            P(axes, None),
        ),
        out_specs=(
            P(axes, None),
            P(axes, None),
            P(axes),
            P(axes, M),
            P(axes, None),
            P(M, axes),
            P(axes),
            P(axes, M),
            P(axes, M),
            P(M, axes),
        ),
        check_vma=False,
    )
```

```python
import functools

import jax
import jax.numpy as jnp
from jax import lax
from jax.experimental import pallas as pl
from jax.experimental.pallas import tpu as pltpu
from jax.sharding import Mesh, PartitionSpec as P

HD = 256
WINDOW = 2048
EPS = 1e-06

PLANES = 4
RANK_SIZES = (2, 4, 2)
RANKS = 16
CHIPS = 8
X = "x"
R = ("yl", "z", "c")
CHIP = ("yl", "z")
CORE = "c"
M = "mp"

F32 = jnp.float32
BF16 = jnp.bfloat16


def after(value, *earlier):
    return lax.optimization_barrier((value,) + earlier)[0]


def rms_scale(values):
    return lax.rsqrt(jnp.mean(values * values, axis=-1, keepdims=True) + EPS)


def norm_back(values, scale_rows, weighted):
    return scale_rows * weighted - values * scale_rows**3 * jnp.mean(
        weighted * values, axis=-1, keepdims=True
    )


def to_plane(block, shift):
    return lax.ppermute(block, X, [(i, (i + shift) % PLANES) for i in range(PLANES)])


def swap(block):
    return lax.ppermute(block, M, [(0, 1), (1, 0)])


def swap_cores(block):
    return lax.ppermute(block, CORE, [(0, 1), (1, 0)])


def rounded(values):
    return lax.reduce_precision(values, 8, 7).astype(BF16)


def sum_mp(part):
    low = rounded(part)
    return low.astype(F32) + swap(low).astype(F32)


def gather_planes(block):
    half = block.shape[0] // 2
    after = to_plane(block, -1)
    before = to_plane(block, 1)
    far_top = to_plane(before[:half], 1)
    far_low = to_plane(after[half:], -1)
    return jnp.concatenate([block, after, far_top, far_low, before], 0)


def collect_planes(block):
    return [block, to_plane(block, 3), to_plane(block, 2), to_plane(block, 1)]


def reduce_far(part):
    rows = part.shape[0] // PLANES
    half = rows // 2
    own, after_one, far, before_one = (
        part[i * rows : (i + 1) * rows].astype(F32) for i in range(PLANES)
    )
    far = rounded(far)
    top = to_plane(far[:half], 1).astype(F32)
    low = to_plane(far[half:], -1).astype(F32)
    after_one = jnp.concatenate([after_one[:half] + top, after_one[half:]], 0)
    before_one = jnp.concatenate([before_one[:half], before_one[half:] + low], 0)
    return own, rounded(after_one), rounded(before_one)


def reduce_near(own, after_one, before_one):
    return own + to_plane(before_one, -1).astype(F32) + to_plane(after_one, 1).astype(F32)


def reduce_planes(part):
    return reduce_near(*reduce_far(part))


def pick(blocks, index):
    return lax.dynamic_index_in_dim(blocks, lax.rem(index + PLANES, PLANES), 0, keepdims=False)


def natural(blocks):
    plane = lax.axis_index(X)
    return [pick(blocks, p - plane) for p in range(PLANES)]


def send_planes(blocks):
    plane = lax.axis_index(X)
    return [pick(blocks, plane)] + [
        to_plane(pick(blocks, plane + k), k) for k in range(1, PLANES)
    ]


def exchange_planes(blocks):
    plane = lax.axis_index(X)
    got = jnp.stack(send_planes(blocks))
    return [pick(got, plane - p) for p in range(PLANES)]


def cut_planes(values):
    rows, width = values.shape
    got = send_planes(values.reshape(rows, PLANES, width // PLANES).swapaxes(0, 1))
    return jnp.concatenate([got[0], got[3], got[2], got[1]], 0)


def cut_features(blocks):
    got = send_planes(blocks)
    return [got[0], got[3], got[2], got[1]]


def join_planes(blocks):
    got = jnp.stack([blocks[0]] + [to_plane(blocks[k], k) for k in range(1, PLANES)])
    plane = lax.axis_index(X)
    return jnp.concatenate([pick(got, plane - p) for p in range(PLANES)], 1)


def permute_features(values):
    rows, width = values.shape
    cut = values.reshape(rows, PLANES, RANKS, width // (PLANES * RANKS))
    return cut.swapaxes(1, 2).reshape(rows, width)


def restore_features(values):
    rows, width = values.shape
    cut = values.reshape(rows, RANKS, PLANES, width // (PLANES * RANKS))
    return cut.swapaxes(1, 2).reshape(rows, width)


def spread(block, axes, size):
    rows, columns = block.shape
    copies = jnp.broadcast_to(block[None], (size, rows, columns)).reshape(size * rows, columns)
    return lax.all_to_all(copies, axes, 0, 0, tiled=True)


def gather_rows(block):
    return lax.all_gather(block, R, axis=0, tiled=True)


def dot_rows(left, right):
    return lax.dot_general(left, right, (((1,), (1,)), ((), ())), preferred_element_type=F32)


def dot_tokens(left, right):
    return lax.dot_general(left, right, (((0,), (0,)), ((), ())), preferred_element_type=F32)


def softmax_parts(query, parts, biases):
    scale = HD ** (-0.5)
    scores = [dot_rows(query, part[0]) * scale + bias[...] for part, bias in zip(parts, biases)]
    top = functools.reduce(
        jnp.maximum, [jnp.max(score, axis=-1, keepdims=True) for score in scores]
    )
    scores = [jnp.exp(score - top) for score in scores]
    inverse = 1.0 / sum(jnp.sum(score, axis=-1, keepdims=True) for score in scores)
    return [score * inverse for score in scores]


def attend_kernel(count, query, *refs):
    parts, biases, out = refs[:count], refs[count : 2 * count], refs[2 * count]
    weights = softmax_parts(query[...], parts, biases)
    out[...] = sum(
        jnp.dot(weight.astype(BF16), part[1], preferred_element_type=F32)
        for weight, part in zip(weights, parts)
    ).astype(out.dtype)


def attend_back_kernel(
    core, query, out_grad, attended, token_scale, *refs
):
    parts, biases, refs = refs[:3], refs[3:6], refs[6:]
    both, window_grad, last_grad, refs = refs[0], refs[1], refs[2], refs[3:]
    queries, out_grads, refs = refs[0], refs[1], refs[2:]
    weights_all, scores_all = refs[:3], refs[3:]
    head = pl.program_id(0)
    heads = pl.num_programs(0)
    rows = query.shape[0]
    here = pl.ds(pl.multiple_of(head * rows, rows), rows)
    scale = HD ** (-0.5)
    weights = softmax_parts(query[...], parts, biases)
    grad = out_grad[...]
    probs = [dot_rows(grad, part[1]) for part in parts]
    inner = sum(
        jnp.sum(weight * prob, axis=-1, keepdims=True) for weight, prob in zip(weights, probs)
    )
    scores = [
        (weight * (prob - inner)).astype(BF16) for weight, prob in zip(weights, probs)
    ]
    both[:, pl.ds(pl.multiple_of(head * HD, HD), HD)] = (
        sum(
            jnp.dot(score, part[0], preferred_element_type=F32)
            for score, part in zip(scores, parts)
        )
        * (token_scale[...] * scale)
    ).astype(both.dtype)
    both[:, pl.ds(pl.multiple_of((heads + head) * HD, HD), HD)] = attended[...]
    queries[here, :] = query[...]
    out_grads[here, :] = grad
    for i in range(3):
        weights_all[i][here, :] = weights[i].astype(BF16)
        scores_all[i][here, :] = scores[i]

    @pl.when(head == heads - 1)
    def _():
        for i in range(3):
            key = (dot_tokens(scores_all[i][...], queries[...]) * scale).astype(BF16)
            value = dot_tokens(weights_all[i][...], out_grads[...]).astype(BF16)
            if i == 2:
                last_grad[0] = key
                last_grad[1] = value
            else:
                which = core[0] if i == 0 else 1 - core[0]
                shape = (CHIPS, 1, rows, HD)
                window_grad[0, :, pl.ds(which, 1)] = key.reshape(shape)
                window_grad[1, :, pl.ds(which, 1)] = value.reshape(shape)


def whole_spec(shape):
    return pl.BlockSpec(shape, lambda i: (0,) * len(shape))


def attend(queries, parts, biases):
    rows, width = queries.shape
    span = sum(bias.shape[1] for bias in biases)
    head_spec = pl.BlockSpec((rows, HD), lambda i: (0, i))
    return pl.pallas_call(
        functools.partial(attend_kernel, len(parts)),
        grid=(width // HD,),
        in_specs=[head_spec] + [whole_spec(v.shape) for v in (*parts, *biases)],
        out_specs=head_spec,
        out_shape=jax.ShapeDtypeStruct(queries.shape, BF16),
        compiler_params=pltpu.CompilerParams(vmem_limit_bytes=48 * 1024 * 1024),
        cost_estimate=pl.CostEstimate(
            flops=4 * rows * width * span,
            bytes_accessed=4 * span * HD + 4 * rows * span + 4 * queries.size,
            transcendentals=rows * span * (width // HD),
        ),
    )(queries, *parts, *biases)


def attend_back(core, queries, out_grad, attended, token_scale, parts, biases):
    rows, width = queries.shape
    heads = width // HD
    spans = [bias.shape[1] for bias in biases]
    head_spec = pl.BlockSpec((rows, HD), lambda i: (0, i))
    shapes = [(rows, 2 * width), (2, CHIPS, 2, rows, HD), parts[-1].shape]
    return pl.pallas_call(
        attend_back_kernel,
        grid=(heads,),
        in_specs=[pl.BlockSpec(memory_space=pltpu.SMEM), head_spec, head_spec, head_spec]
        + [whole_spec(v.shape) for v in (token_scale, *parts, *biases)],
        out_specs=[whole_spec(shape) for shape in shapes],
        out_shape=[jax.ShapeDtypeStruct(shape, BF16) for shape in shapes],
        scratch_shapes=[pltpu.VMEM((heads * rows, HD), BF16)] * 2
        + [pltpu.VMEM((heads * rows, span), BF16) for span in spans] * 2,
        compiler_params=pltpu.CompilerParams(vmem_limit_bytes=56 * 1024 * 1024),
        cost_estimate=pl.CostEstimate(
            flops=10 * rows * width * sum(spans),
            bytes_accessed=8 * sum(spans) * HD + 4 * rows * sum(spans) + 6 * queries.size,
            transcendentals=rows * sum(spans) * heads,
        ),
    )(core.reshape(1), queries, out_grad, attended, token_scale, *parts, *biases)


def geglu_kernel(
    steps, tokens, cot, gate_weight, up_weight, down_weight, hidden, gate_up, grads
):
    step = pl.program_id(0)
    block = gate_weight.shape[1]
    units = hidden.shape[1]

    @pl.when(step < steps)
    def _():
        gate = jnp.dot(tokens[...], gate_weight[...], preferred_element_type=F32)
        up = jnp.dot(tokens[...], up_weight[...], preferred_element_type=F32)
        hidden_grad = jnp.dot(cot[...], down_weight[...], preferred_element_type=F32)
        hidden_grad = hidden_grad.astype(BF16).astype(F32)
        root = 0.7978845608028654
        square = gate * gate
        bend = jnp.tanh(root * gate * (1.0 + 0.044715 * square))
        half = 0.5 * (1.0 + bend)
        gelu = gate * half
        slope = half + 0.5 * gate * (1.0 - bend * bend) * (root * (1.0 + 3 * 0.044715 * square))
        here = pl.ds(pl.multiple_of(step * block, block), block)
        hidden[:, here] = (gelu * up).astype(BF16)
        gate_up[:, here] = (hidden_grad * up * slope).astype(BF16)
        there = pl.ds(pl.multiple_of(units + step * block, block), block)
        gate_up[:, there] = (hidden_grad * gelu).astype(BF16)

    @pl.when(step >= steps)
    def _():
        height = grads.shape[0]
        rows = pl.ds(pl.multiple_of((step - steps) * height, 128), height)
        cut = 512 if units % 512 == 0 else 128
        for left, right, first in ((tokens, gate_up, 0), (cot, hidden, 2 * units)):
            for at in range(0, right.shape[1], cut):
                grads[:, first + at : first + at + cut] = dot_tokens(
                    left[:, rows], right[:, at : at + cut]
                ).astype(BF16)


def geglu(tokens, cot, weights):
    rows, width = tokens.shape
    units = weights.shape[1] // 3
    block = 256 if units % 256 == 0 else 128
    steps = units // block
    height = width // PLANES
    token_spec = pl.BlockSpec(tokens.shape, lambda i: (0, 0), pipeline_mode=pl.Buffered(1))

    def weight_spec(which):
        return pl.BlockSpec(
            (width, block), lambda i: (0, which * steps + jnp.minimum(i, steps - 1))
        )

    return pl.pallas_call(
        functools.partial(geglu_kernel, steps),
        grid=(steps + PLANES,),
        in_specs=[token_spec, token_spec] + [weight_spec(which) for which in range(3)],
        out_specs=[
            whole_spec((rows, units)),
            whole_spec((rows, 2 * units)),
            pl.BlockSpec((height, 3 * units), lambda i: (jnp.maximum(i - steps, 0), 0)),
        ],
        out_shape=[
            jax.ShapeDtypeStruct((rows, units), BF16),
            jax.ShapeDtypeStruct((rows, 2 * units), BF16),
            jax.ShapeDtypeStruct((width, 3 * units), BF16),
        ],
        compiler_params=pltpu.CompilerParams(vmem_limit_bytes=60 * 1024 * 1024),
        cost_estimate=pl.CostEstimate(
            flops=4 * rows * width * 3 * units,
            bytes_accessed=4 * weights.size + 4 * tokens.size + 6 * rows * units,
            transcendentals=rows * units,
        ),
    )(tokens, cot, weights, weights, weights)


def outer_kernel(count, *refs):
    out = refs[-1]
    first = 0
    for i in range(count):
        left, right = refs[2 * i], refs[2 * i + 1]
        columns = right.shape[1]
        tokens_first = left.shape[0] == right.shape[0]
        step = 512 if columns % 512 == 0 else columns
        for at in range(0, columns, step):
            out[:, first + at : first + at + step] = lax.dot_general(
                left[...],
                right[:, at : at + step],
                (((0 if tokens_first else 1,), (0,)), ((), ())),
                preferred_element_type=F32,
            ).astype(out.dtype)
        first += columns


def token_outer(*pairs):
    tokens, height = pairs[0][0].shape
    columns = sum(right.shape[1] for _, right in pairs)
    block = next(size for size in (512, 640, 256, 128) if height % size == 0)
    specs, operands = [], []
    for left, right in pairs:
        specs += [
            pl.BlockSpec((tokens, block), lambda i: (0, i))
            if left.shape[0] == tokens
            else pl.BlockSpec((block, tokens), lambda i: (i, 0)),
            pl.BlockSpec(right.shape, lambda i: (0, 0)),
        ]
        operands += [left, right]
    return pl.pallas_call(
        functools.partial(outer_kernel, len(pairs)),
        grid=(height // block,),
        in_specs=specs,
        out_specs=pl.BlockSpec((block, columns), lambda i: (i, 0)),
        out_shape=jax.ShapeDtypeStruct((height, columns), BF16),
        compiler_params=pltpu.CompilerParams(vmem_limit_bytes=40 * 1024 * 1024),
        cost_estimate=pl.CostEstimate(
            flops=2 * tokens * height * columns,
            bytes_accessed=2 * height * columns + 2 * tokens * (height * len(pairs) + columns),
            transcendentals=0,
        ),
    )(*operands)


def attn_outer_kernel(*refs):
    inputs, cuts, boths = refs[0], refs[1:5], refs[5:9]
    out = refs[9]
    rows, width = boths[0].shape[0], boths[0].shape[1] // 2
    out[:, :width] = sum(
        dot_tokens(inputs[k * rows : (k + 1) * rows, :], boths[k][:, :width])
        for k in range(PLANES)
    ).astype(out.dtype)
    out[:, width:] = sum(
        jnp.dot(cuts[k][...], boths[k][:, width:], preferred_element_type=F32)
        for k in range(PLANES)
    ).astype(out.dtype)


def attn_outer(inputs, cuts, boths):
    height, columns = inputs.shape[1], boths[0].shape[1]
    rows = boths[0].shape[0]
    block = 128
    return pl.pallas_call(
        attn_outer_kernel,
        grid=(height // block,),
        in_specs=[pl.BlockSpec((inputs.shape[0], block), lambda i: (0, i))]
        + [pl.BlockSpec((block, rows), lambda i: (i, 0))] * PLANES
        + [whole_spec(boths[0].shape)] * PLANES,
        out_specs=pl.BlockSpec((block, columns), lambda i: (i, 0)),
        out_shape=jax.ShapeDtypeStruct((height, columns), BF16),
        compiler_params=pltpu.CompilerParams(vmem_limit_bytes=40 * 1024 * 1024),
        cost_estimate=pl.CostEstimate(
            flops=2 * PLANES * rows * height * columns,
            bytes_accessed=2 * (height + PLANES * rows) * columns + 4 * inputs.size,
            transcendentals=0,
        ),
    )(inputs, *cuts, *boths)


def input_back_kernel(*refs):
    boths, keyvals, query_rows, keyval_rows = refs[:4], refs[4:8], refs[8], refs[9]
    keyval_out, outs = refs[10], refs[11:]
    rows, width = boths[0].shape[0], boths[0].shape[1] // 2
    for k in range(PLANES):
        keyval = (
            keyvals[k][:rows].astype(F32) + keyvals[(k + 1) % PLANES][rows:].astype(F32)
        ).astype(BF16)
        keyval_out[k * rows : (k + 1) * rows] = keyval
        outs[k][...] = (
            dot_rows(boths[k][:, :width], query_rows[...]) + dot_rows(keyval, keyval_rows[...])
        ).astype(outs[k].dtype)


def input_back(boths, keyvals, query_rows, keyval_rows):
    rows = boths[0].shape[0]
    height = query_rows.shape[0]
    shapes = [(PLANES * rows, HD)] + [(rows, height)] * PLANES
    operands = (*boths, *keyvals, query_rows, keyval_rows)
    return pl.pallas_call(
        input_back_kernel,
        grid=(1,),
        in_specs=[whole_spec(v.shape) for v in operands],
        out_specs=[whole_spec(shape) for shape in shapes],
        out_shape=[jax.ShapeDtypeStruct(shape, BF16) for shape in shapes],
        compiler_params=pltpu.CompilerParams(vmem_limit_bytes=40 * 1024 * 1024),
        cost_estimate=pl.CostEstimate(
            flops=2 * PLANES * rows * height * query_rows.shape[1],
            bytes_accessed=2 * sum(v.size for v in operands) + 2 * PLANES * rows * height,
            transcendentals=0,
        ),
    )(*operands)


def join_kernel(padded, gate_weight, up_weight, gain, *refs):
    pieces, outs, gain_out = refs[:PLANES], refs[PLANES : PLANES + 3], refs[PLANES + 3]
    units = gate_weight.shape[1] // PLANES
    total = jnp.zeros((gate_weight.shape[0], 1), F32)
    for p in range(PLANES):
        columns = slice(p * units, (p + 1) * units)
        gate = pieces[p][:, :units].astype(F32)
        up = pieces[p][:, padded : padded + units].astype(F32)
        total += jnp.sum(
            gate_weight[:, columns].astype(F32) * gate + up_weight[:, columns].astype(F32) * up,
            axis=1,
            keepdims=True,
        )
        outs[0][:, columns] = gate * gain[...]
        outs[1][:, columns] = up * gain[...]
        outs[2][:, columns] = pieces[p][:, 2 * padded : 2 * padded + units].astype(F32)
    gain_out[...] = total


def join(pieces, gate_weight, up_weight, gain):
    shape = gate_weight.shape
    padded = pieces[0].shape[1] // 3
    operands = (gate_weight, up_weight, gain, *pieces)
    shapes = [shape] * 3 + [(shape[0], 1)]
    return pl.pallas_call(
        functools.partial(join_kernel, padded),
        grid=(1,),
        in_specs=[whole_spec(v.shape) for v in operands],
        out_specs=[whole_spec(one) for one in shapes],
        out_shape=[jax.ShapeDtypeStruct(one, F32) for one in shapes],
        compiler_params=pltpu.CompilerParams(vmem_limit_bytes=40 * 1024 * 1024),
        cost_estimate=pl.CostEstimate(
            flops=10 * gate_weight.size,
            bytes_accessed=24 * gate_weight.size,
            transcendentals=0,
        ),
    )(*operands)


def body(
    inputs,
    attn_gain,
    query_weight,
    keyval_weight,
    out_weight,
    ffn_gain,
    gate_weight,
    up_weight,
    down_weight,
    positions,
    cotangent,
):
    rows, width = inputs.shape
    own = attn_gain.shape[0]
    query_width = query_weight.shape[1]
    head_count = query_width // HD
    units = gate_weight.shape[1] // PLANES
    padded = -(-units // 128) * 128
    scale = HD ** (-0.5)
    plane = lax.axis_index(X)
    rank = lax.axis_index(R)
    half = lax.axis_index(M)
    core = lax.axis_index(CORE)
    chip = lax.axis_index(CHIP)
    chips = jnp.arange(CHIPS, dtype=jnp.int32)
    ahead = (chips >= chip)[:, None, None]
    at_home = (chips == chip)[:, None, None]
    gain_one = attn_gain.astype(F32)[:, None]
    gain_two = ffn_gain.astype(F32)[:, None]

    keyval_own = (
        lax.dynamic_slice_in_dim(keyval_weight, half * HD, HD, 1).astype(F32) * gain_one
    ).astype(BF16)
    query_own = (query_weight.astype(F32) * gain_one).astype(BF16)
    inputs_cut = cut_planes(inputs)
    tokens_in = inputs.astype(F32)
    scale_attn = rms_scale(tokens_in)
    scale_before = to_plane(scale_attn.reshape(1, rows), 1).reshape(rows, 1)

    def cut(weight):
        blocks = weight.reshape(own, PLANES, units)
        return jnp.pad(blocks, ((0, 0), (0, 0), (0, padded - units))).swapaxes(0, 1)

    ffn_own = jnp.concatenate(
        [
            cut((gate_weight.astype(F32) * gain_two).astype(BF16)),
            cut((up_weight.astype(F32) * gain_two).astype(BF16)),
            cut(down_weight.T),
        ],
        2,
    ).reshape(PLANES * own, 3 * padded)
    out_planes = lax.all_gather(out_weight.T, X, axis=0, tiled=True)
    both = gather_rows(jnp.concatenate([query_own, out_planes], 0))
    ffn_own = lax.all_to_all(after(ffn_own, out_planes), X, 0, 0, tiled=True)
    ffn = gather_rows(ffn_own)
    keyval_rows = spread(after(keyval_own, ffn_own), R, RANKS)

    ranks = jnp.arange(RANKS, dtype=jnp.int32)
    block_own = plane * RANKS + rank
    offsets = jnp.arange(rows, dtype=jnp.int32)
    span = RANKS * rows
    pos_own = lax.dynamic_slice_in_dim(positions, plane * span, span, 0).reshape(RANKS, rows)
    pos_before = lax.dynamic_slice_in_dim(
        positions, jnp.maximum(plane - 1, 0) * span, span, 0
    ).reshape(RANKS, rows)
    pos_last = lax.dynamic_slice_in_dim(pos_before, rank, 1, 0)
    def in_parts(own_values, before_values, last_values):
        chosen = jnp.where((ranks <= rank)[:, None], own_values, before_values)
        cores = chosen.reshape(CHIPS, 2, rows)
        parts = [
            lax.dynamic_index_in_dim(cores, index, 1, keepdims=False).reshape(-1)
            for index in (core, 1 - core)
        ]
        return jnp.concatenate(parts + [last_values.reshape(-1)])

    index_own = ((plane * RANKS + ranks) * rows)[:, None] + offsets[None]
    key_index = in_parts(
        index_own, index_own - span, (block_own - RANKS) * rows + offsets
    )
    pos_keys = in_parts(pos_own, pos_before, pos_last)
    pos_query = lax.dynamic_slice_in_dim(positions, block_own * rows, rows, 0)
    query_index = block_own * rows + offsets
    allowed = (
        (key_index[None, :] >= 0)
        & (key_index[None, :] <= query_index[:, None])
        & (pos_query[:, None] - pos_keys[None, :] < WINDOW)
    )

    bias = jnp.where(allowed, 0.0, -1e30)
    part_span = CHIPS * rows
    biases = [
        bias[:, :part_span],
        bias[:, part_span : 2 * part_span],
        bias[:, 2 * part_span :],
    ]
    residual, cot = lax.optimization_barrier(
        (
            permute_features(after(inputs, ffn_own)),
            permute_features(after(cotangent, ffn_own)),
        )
    )

    keyval = (
        reduce_planes(
            jnp.dot(
                after(inputs_cut, residual, cot),
                keyval_rows,
                preferred_element_type=F32,
            )
        )
        * scale_attn
    ).astype(BF16)
    keyval_before = to_plane(keyval, 1)
    before_other = to_plane(swap(keyval), 1)
    down = ffn[:, 2 * padded :]

    both = both.reshape(RANKS, (1 + PLANES) * own, query_width)
    query_rows = lax.optimization_barrier(both[:, :own].reshape(RANKS * own, query_width))
    out_rows = both[:, own:].reshape(width, query_width)
    queries_part = jnp.dot(after(inputs_cut, before_other), query_rows, preferred_element_type=F32)
    queries_sum = reduce_planes(queries_part)
    first = half == 0
    last = jnp.where(
        first,
        jnp.stack([keyval_before, before_other]),
        jnp.stack([before_other, keyval_before]),
    )
    chosen = jnp.where(ahead, keyval[None], keyval_before[None])
    sent = jnp.broadcast_to(chosen[None], (2, CHIPS, rows, HD))
    met = lax.all_to_all(
        sent.reshape(2 * CHIPS * rows, HD), (M,) + CHIP, 0, 0, tiled=True
    ).reshape(2, CHIPS, rows, HD)
    met_lent = jnp.where(at_home & (core == 1), last[:, None], met)
    met_other = swap_cores(after(met_lent, queries_sum))
    window = [v.reshape(2, CHIPS * rows, HD) for v in (met, met_other)]
    queries, out_rows = lax.optimization_barrier(
        ((queries_sum * scale_attn).astype(BF16), out_rows)
    )

    attended = attend(queries, window + [last], biases)
    branch_part = jnp.einsum("te,de->td", attended, out_rows, preferred_element_type=F32)
    branch = sum_mp(branch_part)
    cot_all = gather_planes(after(cot, queries))
    middle = residual.astype(F32) + after(branch, cot_all)

    scale_ffn = rms_scale(middle)
    normed = (middle * scale_ffn).astype(BF16)
    normed_all = gather_planes(normed)
    hidden, gate_up_low, ffn_grad_part = geglu(normed_all, cot_all, ffn)
    ffn_grad_rows = lax.psum_scatter(ffn_grad_part, R, scatter_dimension=0, tiled=True)
    weighted_part = jnp.einsum(
        "tf,ef->te", gate_up_low, ffn[:, : 2 * padded], preferred_element_type=F32
    ).astype(BF16)
    weighted_low = rounded(reduce_planes(weighted_part))
    weighted = weighted_low.astype(F32) + swap(weighted_low).astype(F32)

    middle_grad = cot.astype(F32) + norm_back(middle, scale_ffn, weighted)
    branch_low = middle_grad.astype(BF16)
    attended_grad = jnp.dot(branch_low, out_rows, preferred_element_type=F32).astype(BF16)
    query_both, window_grad, last_grad = attend_back(
        core, queries, attended_grad, attended, scale_attn, window + [last], biases
    )
    gathered = collect_planes(query_both)
    branch_late = after(branch_low, *gathered)
    branch_turned = branch_late.T.reshape(RANKS, PLANES, own, rows)
    branch_cut = cut_features(branch_turned.swapaxes(0, 1).reshape(PLANES, RANKS * own, rows))

    ffn_part = jnp.einsum(
        "tf,ef->te", after(hidden, *branch_cut), down, preferred_element_type=F32
    )
    ffn_low = rounded(reduce_planes(ffn_part))

    returned = lax.all_to_all(
        window_grad.reshape(2 * RANKS * rows, HD), (M,) + R, 0, 0, tiled=True
    ).reshape(2, RANKS, rows, HD)
    last_other = swap(jnp.where(first, last_grad[1], last_grad[0]))
    last_mine = jnp.where(first, last_grad[0], last_grad[1])
    own_plane = (ranks >= rank)[:, None, None]
    own_sum = jnp.sum(jnp.where(own_plane, returned, 0).astype(F32), (0, 1))
    before_sum = (
        jnp.sum(jnp.where(own_plane, 0, returned).astype(F32), (0, 1))
        + last_mine.astype(F32)
        + last_other.astype(F32)
    )

    keyval_pieces = collect_planes(
        rounded(jnp.concatenate([own_sum * scale_attn, before_sum * scale_before], 0))
    )
    attn_grad_part = attn_outer(inputs_cut, branch_cut, gathered)
    attn_width = attn_grad_part.shape[1]
    attn_cores = attn_grad_part.reshape(CHIPS, 2, own, attn_width)
    attn_lent = swap_cores(lax.dynamic_index_in_dim(attn_cores, 1 - core, 1, keepdims=False))
    attn_kept = lax.dynamic_index_in_dim(attn_cores, core, 1, keepdims=False)
    attn_chip = rounded(attn_kept.astype(F32) + attn_lent.astype(F32))
    attn_met = lax.all_to_all(
        attn_chip.reshape(CHIPS * own, attn_width), CHIP, 0, 0, tiled=True
    )
    keyval_all, *input_parts = input_back(gathered, keyval_pieces, query_rows, keyval_rows)
    ffn_grad_rows, middle_late, ffn_low, attn_met = lax.optimization_barrier(
        (ffn_grad_rows, middle_grad, ffn_low, attn_met)
    )
    weighted_low = after(rounded(join_planes(input_parts).astype(F32)), attn_met)
    weighted_other = swap(weighted_low)
    ffn_grad_rows = after(ffn_grad_rows, weighted_low)
    attn_base = jnp.sum(attn_met.reshape(CHIPS, own, attn_width).astype(F32), 0)
    query_base = attn_base[:, :query_width]
    out_weight_grad = attn_base[:, query_width : 2 * query_width].T
    keyval_met = lax.all_to_all(
        after(token_outer((inputs_cut, keyval_all)), attn_met), R, 0, 0, tiled=True
    )
    keyval_mine = jnp.sum(keyval_met.reshape(RANKS, own, HD).astype(F32), 0)
    keyval_other = swap(after(keyval_mine, weighted_other))
    keyval_base = jnp.concatenate(
        [
            jnp.where(first, keyval_mine, keyval_other),
            jnp.where(first, keyval_other, keyval_mine),
        ],
        1,
    )

    weighted_one = weighted_low.astype(F32) + weighted_other.astype(F32)
    input_grad = (
        restore_features(middle_late)
        + weighted_one
        - tokens_in
        * scale_attn**2
        * jnp.mean(weighted_one * tokens_in, axis=-1, keepdims=True)
    )

    ffn_low = restore_features(ffn_low)
    ffn_other = swap(ffn_low)
    ffn_sum = ffn_low.astype(F32) + ffn_other.astype(F32)
    activations = (restore_features(middle) + ffn_sum).astype(BF16)
    ffn_grad_own = exchange_planes(ffn_grad_rows.reshape(PLANES, own, 3 * padded))
    ffn_grad_own[0] = after(ffn_grad_own[0], ffn_other)
    gate_weight_grad, up_weight_grad, down_rows, ffn_gain_part = join(
        ffn_grad_own, gate_weight, up_weight, gain_two
    )

    gain_parts = jnp.stack(
        [jnp.sum(query_weight.astype(F32) * query_base, axis=1), ffn_gain_part[:, 0]]
    )
    gain_sums = gain_parts + swap(after(gain_parts, weighted_other))
    ffn_gain_grad = gain_sums[1]
    attn_gain_grad = gain_sums[0] + jnp.sum(keyval_weight.astype(F32) * keyval_base, axis=1)

    return (
        activations,
        input_grad,
        attn_gain_grad,
        query_base * gain_one,
        keyval_base * gain_one,
        out_weight_grad,
        ffn_gain_grad,
        gate_weight_grad,
        up_weight_grad,
        down_rows.T,
    )


def solution(mesh):
    axes = (X,) + R
    cut = Mesh(mesh.devices.reshape((PLANES,) + RANK_SIZES + (2,)), axes + (M,))
    return jax.shard_map(
        body,
        mesh=cut,
        in_specs=(
            P(axes, None),
            P(axes),
            P(axes, M),
            P(axes, None),
            P(M, axes),
            P(axes),
            P(axes, M),
            P(axes, M),
            P(M, axes),
            P(),
            P(axes, None),
        ),
        out_specs=(
            P(axes, None),
            P(axes, None),
            P(axes),
            P(axes, M),
            P(axes, None),
            P(M, axes),
            P(axes),
            P(axes, M),
            P(axes, M),
            P(M, axes),
        ),
        check_vma=False,
    )
```
